128 devices in a mesh: dp: 16 (over z, y), tensor: 8 (over x, core).
Axes of the slice: x: 4, y: 4, z: 4, core: 2. Of those that a mesh axis runs over, the one named last changes fastest.
Arguments:
- tokens: bfloat16 [1024, 8192], P('tensor', 'dp'), may hold values from -6 to 6
- gate_int_codes: bfloat16 [8192, 26624], P('dp', 'tensor'), may hold values from -8 to 7, as said below
- up_int_codes: bfloat16 [8192, 26624], P('dp', 'tensor'), may hold values from -8 to 7, as said below
- down_int_codes: bfloat16 [26624, 8192], P('tensor', 'dp'), may hold values from -8 to 7, as said below
- gate_column_scale: float32 [26624], P('tensor'), may hold values from 0.0006629126 to 0.006629126
- up_column_scale: float32 [26624], P('tensor'), may hold values from 0.0006629126 to 0.006629126
- down_column_scale: float32 [8192], P('dp'), may hold values from 0.00036771776 to 0.0036771775
- row_adapter_index: int32 [1024], replicated, may hold values from 0 to 255
- adapter_shrink_weight: bfloat16 [256, 26624, 16], P('dp', 'tensor'), may hold values from -0.0390625 to 0.0390625
- adapter_expand_weight: bfloat16 [256, 16, 8192], P(None, None, 'dp'), may hold values from -1.5 to 1.5
Outputs:
- layer_out: bfloat16 [1024, 8192], P('tensor', 'dp')
The draws below stay inside these ranges and needn't reach their ends.
Inputs may be any that keep to these rules, and one draw needn't show every extreme that they name: `gate_int_codes`: every entry is a whole number. `up_int_codes`: every entry is a whole number. `down_int_codes`: every entry is a whole number.
All inputs are finite; a program needn't handle non-finite values.
Results may differ from the reference program's by a relative error of at most 0.03.
Values may be sent and summed in bfloat16 or wider, within the bound.
A program may use at most 192 MiB of HBM per device.

```python
import math
import jax
import jax.numpy as jnp
import numpy as np
from jax import lax

MODEL_WIDTH = 8192
HIDDEN_UNITS = 26624
FACTOR = 13
ADAPTER_COUNT = 256
ADAPTER_RANK = 16
ROWS = 1024
N_DP = 16
N_TENSOR = 8


def draw_gate_int_codes(key, part):
    key = jax.random.fold_in(key, 11)
    return jax.random.randint(key, (MODEL_WIDTH, HIDDEN_UNITS), -8, 8, dtype=jnp.int32).astype(jnp.bfloat16)


def draw_up_int_codes(key, part):
    key = jax.random.fold_in(key, 23)
    return jax.random.randint(key, (MODEL_WIDTH, HIDDEN_UNITS), -8, 8, dtype=jnp.int32).astype(jnp.bfloat16)


def draw_down_int_codes(key, part):
    key = jax.random.fold_in(key, 37)
    return jax.random.randint(key, (HIDDEN_UNITS, MODEL_WIDTH), -8, 8, dtype=jnp.int32).astype(jnp.bfloat16)


def with_ends(result, own_key, smallest, high):
    spot = [jax.random.randint(jax.random.fold_in(own_key, axis), (), 0, length) for axis, length in enumerate(result.shape)]
    main_axis = result.shape.index(max(result.shape))
    next_to = spot[:main_axis] + [(spot[main_axis] + 1) % result.shape[main_axis]] + spot[main_axis + 1:]
    return result.at[tuple(spot)].set(smallest).at[tuple(next_to)].set(high)


def shard_levels(own_key, shape, shards, smallest, high):
    gain, own = 1.0, jax.random.fold_in(own_key, 6)
    for dim, blocks in shards:
        draws = jnp.exp(jax.random.uniform(jax.random.fold_in(own, dim), (blocks,), jnp.float32, smallest / len(shards), high / len(shards)))
        gain = gain * jnp.repeat(draws, shape[dim] // blocks).reshape([-1 if axis == dim else 1 for axis in range(len(shape))])
    return gain


def rank_table(amount, slope):
    loads = [(1 << 20) // math.isqrt(grade ** slope) + 1 for grade in range(1, amount + 1)]
    width = 1 + sum(loads) // (1 << 30)
    return np.cumsum(np.array([max(1, weight // width) for weight in loads]))


def skewed_ids(stream_key, extent, count, slope):
    listing = rank_table(count, slope)
    ticket = jax.random.randint(jax.random.fold_in(stream_key, 1), extent, 0, int(listing[count - 1]))
    standing = jnp.searchsorted(jnp.asarray(listing, jnp.int32), ticket, side="right")
    return jax.random.permutation(jax.random.fold_in(stream_key, 2), count)[standing].astype(jnp.int32)


def noise(key, shape, deviation, bound, pieces=(), held_as=jnp.bfloat16):
    values = deviation * jax.random.normal(key, shape, jnp.float32)
    if pieces:
        values = values * shard_levels(key, shape, pieces, -0.22, 0.18)
    return jnp.clip(values, -bound, bound).astype(held_as)


def setup_inputs(seed: int = 0) -> dict:
    seeds = jax.random.split(jax.random.key(seed), 11)
    return {
        "tokens": noise(seeds[0], (ROWS, MODEL_WIDTH), 1.0, 6.0, ((0, 8), (1, 16))),
        "gate_int_codes": draw_gate_int_codes(jax.random.fold_in(seeds[10], 71), 0),
        "up_int_codes": draw_up_int_codes(jax.random.fold_in(seeds[10], 71), 0),
        "down_int_codes": draw_down_int_codes(jax.random.fold_in(seeds[10], 71), 0),
        "gate_column_scale": jnp.clip(jnp.exp(math.log(0.006629126) - 2.3025851 * jax.random.uniform(seeds[4], (HIDDEN_UNITS,), jnp.float32) ** shard_levels(seeds[4], (HIDDEN_UNITS,), ((0, 8),), -0.2, 0.2)), 0.0006629126, 0.006629126),
        "up_column_scale": jnp.clip(jnp.exp(math.log(0.006629126) - 2.3025851 * jax.random.uniform(seeds[5], (HIDDEN_UNITS,), jnp.float32) ** shard_levels(seeds[5], (HIDDEN_UNITS,), ((0, 8),), -0.2, 0.2)), 0.0006629126, 0.006629126),
        "down_column_scale": jnp.clip(jnp.exp(math.log(0.0036771775) - 2.3025851 * jax.random.uniform(seeds[6], (MODEL_WIDTH,), jnp.float32) ** shard_levels(seeds[6], (MODEL_WIDTH,), ((0, 16),), -0.2, 0.2)), 0.00036771776, 0.0036771775),
        "row_adapter_index": with_ends(skewed_ids(seeds[7], (ROWS,), ADAPTER_COUNT, 2), jax.random.fold_in(seeds[7], 3), 0, ADAPTER_COUNT - 1).astype(jnp.int32),
        "adapter_shrink_weight": noise(seeds[8], (ADAPTER_COUNT, HIDDEN_UNITS, ADAPTER_RANK), HIDDEN_UNITS ** -0.5, 0.0390625, ((0, 16), (1, 8))),
        "adapter_expand_weight": noise(seeds[9], (ADAPTER_COUNT, ADAPTER_RANK, MODEL_WIDTH), ADAPTER_RANK ** -0.5, 1.5, ((2, 16),)),
    }


def sylvester(mat_order):
    indices = jnp.arange(mat_order, dtype=jnp.int32)
    common = jnp.bitwise_and(indices[:, None], indices[None, :])
    parity = jnp.zeros((mat_order, mat_order), jnp.int32)
    for bit_pos in range(max(mat_order.bit_length() - 1, 0)):
        parity = parity + jnp.bitwise_and(jnp.right_shift(common, bit_pos), 1)
    parity = jnp.bitwise_and(parity, 1)
    return (1 - 2 * parity).astype(jnp.float32) / jnp.float32(math.sqrt(mat_order))

def hartley(mat_order):
    indices = jnp.arange(mat_order, dtype=jnp.int32)
    product = indices[:, None] * indices[None, :] % mat_order
    angles = product.astype(jnp.float32) * jnp.float32(2.0 * math.pi / mat_order)
    return (jnp.cos(angles) + jnp.sin(angles)) / jnp.float32(math.sqrt(mat_order))

def dequant(codes, scale):
    return (codes.astype(jnp.float32) * scale).astype(jnp.bfloat16)

def reference(tokens, gate_int_codes, up_int_codes, down_int_codes, gate_column_scale, up_column_scale, down_column_scale, row_adapter_index, adapter_shrink_weight, adapter_expand_weight):
    highest = lax.Precision.HIGHEST
    block_len = MODEL_WIDTH // N_DP

    def add_block(carry, block_id):
        start = (block_id * block_len).astype(jnp.int32)
        rows_in = lax.dynamic_slice_in_dim(tokens, start, block_len, 1)
        gate_w = dequant(lax.dynamic_slice_in_dim(gate_int_codes, start, block_len, 0), gate_column_scale)
        up_w = dequant(lax.dynamic_slice_in_dim(up_int_codes, start, block_len, 0), up_column_scale)
        gate_term = jnp.dot(rows_in, gate_w, preferred_element_type=jnp.float32).astype(jnp.bfloat16)
        up_term = jnp.dot(rows_in, up_w, preferred_element_type=jnp.float32).astype(jnp.bfloat16)
        gate_term, up_term = lax.optimization_barrier((gate_term, up_term))
        return ((carry[0] + gate_term.astype(jnp.float32), carry[1] + up_term.astype(jnp.float32)), None)
    zeros_init = jnp.zeros((ROWS, HIDDEN_UNITS), jnp.float32)
    totals, unused = lax.scan(add_block, (zeros_init, zeros_init), jnp.arange(N_DP, dtype=jnp.int32))
    hidden = jax.nn.silu(totals[0]) * totals[1]
    local_len = HIDDEN_UNITS // (N_TENSOR * FACTOR)
    shaped = hidden.reshape(ROWS, N_TENSOR, FACTOR, local_len)
    shaped = jnp.einsum('rtad,ed->rtae', shaped, sylvester(local_len), precision=highest)
    shaped = jnp.einsum('rtad,ba->rtbd', shaped, hartley(FACTOR), precision=highest)
    shaped = jnp.einsum('rtad,st->rsad', shaped, sylvester(N_TENSOR), precision=highest)
    rotated = shaped.reshape(ROWS, HIDDEN_UNITS).astype(jnp.bfloat16)
    hidden_len = HIDDEN_UNITS // N_TENSOR

    def add_down(carry, block_id):
        start = (block_id * hidden_len).astype(jnp.int32)
        cols_in = lax.dynamic_slice_in_dim(rotated, start, hidden_len, 1)
        down_w = dequant(lax.dynamic_slice_in_dim(down_int_codes, start, hidden_len, 0), down_column_scale)
        return (carry + jnp.dot(cols_in, down_w, preferred_element_type=jnp.float32), None)
    base, unused = lax.scan(add_down, jnp.zeros((ROWS, MODEL_WIDTH), jnp.float32), jnp.arange(N_TENSOR, dtype=jnp.int32))

    def shrink_row(pair):
        row_vals, selector_mask = pair
        square_matrix = lax.dynamic_index_in_dim(adapter_shrink_weight, selector_mask, 0, keepdims=False)
        return jnp.dot(row_vals.astype(jnp.float32), square_matrix.astype(jnp.float32), precision=highest)
    shrunk_rows = lax.map(shrink_row, (rotated, row_adapter_index))
    selected_rows = jnp.take(adapter_expand_weight, row_adapter_index, axis=0)
    extra = jnp.einsum('rk,rkd->rd', shrunk_rows, selected_rows.astype(jnp.float32), precision=highest)
    return (base + extra).astype(jnp.bfloat16)
```

```python
import math

import jax
import jax.numpy as jnp
import numpy as np
from jax import lax
from jax.experimental import pallas as pl
from jax.experimental.pallas import tpu as pltpu
from jax.sharding import PartitionSpec as P

FACTOR = 13
ADAPTER_RANK = 16
MESH = pl.DeviceIdType.MESH
F32, BF16 = jnp.float32, jnp.bfloat16


def sylvester_signs(order):
    i = np.arange(order)
    common = i[:, None] & i[None, :]
    parity = np.zeros_like(common)
    while common.any():
        parity ^= common & 1
        common = common >> 1
    return 1 - 2 * parity


def hartley_entries(order):
    i = np.arange(order)
    angle = 2.0 * np.pi * ((i[:, None] * i[None, :]) % order) / order
    return (np.cos(angle) + np.sin(angle)) / math.sqrt(order)


def order_of(j):
    return (2 - j + (j // 2) * (7 - 2 * j)) % 4


def first_kernel(
    tok, wg_hbm, wu_hbm, sg, su, signs, out,
    xb, wg, wu, p, r1, r2, t1, t2, hid, mid,
    load_sem, gs, gr, s1s, s1r, s2s, s2r,
):
    dp, tensor = lax.axis_index("dp"), lax.axis_index("tensor")
    z, y = dp // 4, dp % 4
    x, core = tensor // 2, tensor % 2
    cols = wg.shape[1]

    def at_x(step, c):
        return (dp, ((x + step) % 4) * 2 + c)

    def at_z(step):
        return (((z + step) % 4) * 4 + y, tensor)

    def at_y(step):
        return (z * 4 + (y + step) % 4, tensor)

    loads = [
        pltpu.make_async_copy(tok, xb.at[x, pl.ds(2 * core, 2)], load_sem.at[0]),
        pltpu.make_async_copy(wg_hbm, wg, load_sem.at[1]),
        pltpu.make_async_copy(wu_hbm, wu, load_sem.at[2]),
    ]
    for load in loads:
        load.start()

    near = [at_x(0, 1 - core), at_x(1, core), at_x(3, core), at_z(1), at_z(3), at_y(1), at_y(3)]
    barrier = pltpu.get_barrier_semaphore()
    for who in near:
        pl.semaphore_signal(barrier, inc=1, device_id=who, device_id_type=MESH)
    pl.semaphore_wait(barrier, len(near))

    def remote(src, dst, send, recv, who):
        return pltpu.make_async_remote_copy(
            src_ref=src, dst_ref=dst, send_sem=send, recv_sem=recv, device_id=who, device_id_type=MESH
        )

    def shard(step, c):
        return xb.at[(x + step) % 4, pl.ds(2 * c, 2)]

    def part(step, c, h):
        return xb.at[(x + step) % 4, 2 * c + h]

    mate = at_x(0, 1 - core)

    def gather_copy(i, src, dst, who):
        return remote(src, dst, gs.at[i], gr.at[i], who)

    g_sends = [
        gather_copy(0, tok, shard(0, core), mate),
        gather_copy(1, tok, shard(0, core), at_x(1, core)),
        gather_copy(2, tok, shard(0, core), at_x(3, core)),
    ]
    for c in g_sends:
        c.start()

    def landed(i, ref):
        gather_copy(i, ref, ref, mate).wait_recv()

    def pass_on(i, ref, who):
        c = gather_copy(i, ref, ref, who)
        c.start()
        g_sends.append(c)

    landed(1, shard(3, core))
    pass_on(3, part(3, core, 0), at_x(1, core))
    pass_on(5, shard(3, core), mate)
    landed(2, shard(1, core))
    pass_on(4, part(1, core, 1), at_x(3, core))
    pass_on(6, shard(1, core), mate)
    landed(3, part(2, core, 0))
    pass_on(7, part(2, core, 0), mate)
    landed(4, part(2, core, 1))
    pass_on(8, part(2, core, 1), mate)
    for load in loads:
        load.wait()
    landed(0, shard(0, 1 - core))
    landed(5, shard(3, 1 - core))
    landed(6, shard(1, 1 - core))
    landed(7, part(2, 1 - core, 0))
    landed(8, part(2, 1 - core, 1))

    first, second = (z, y), (y, z)
    along = ((at_z, at_y), (at_y, at_z))

    def rows(h):
        return pl.ds(pl.multiple_of(32 * h, 32), 32)

    def stage1(m, s, kind, k):
        step = 1 + 2 * s
        b = (second[m] + order_of(k)) % 4
        a = (first[m] + (2 if kind == 0 else step)) % 4
        h = 1 - s if kind == 1 else s
        src = p.at[m, a, b, rows(h)]
        dst = r1.at[m, s, b] if kind == 0 else r2.at[m, s, b, rows(h)]
        return remote(src, dst, s1s.at[m, s, kind, k], s1r.at[m, s, kind, k], along[m][0](step))

    def stage2(m, s, kind):
        step = 1 + 2 * s
        b = (second[m] + (2 if kind == 0 else step)) % 4
        h = 1 - s if kind == 1 else s
        src = p.at[m, first[m], b, rows(h)]
        dst = t1.at[m, s] if kind == 0 else t2.at[m, s, rows(h)]
        return remote(src, dst, s2s.at[m, s, kind], s2r.at[m, s, kind], along[m][1](step))

    def each(count, do):
        lax.fori_loop(0, count, lambda i, carry: (do(i), carry)[1], 0)

    def chunk(j):
        for m, w in ((0, wg), (1, wu)):
            a = (first[m] + order_of(j)) % 4
            xs = (xb[a] if m == 0 else xb[:, a]).reshape(256, xb.shape[-1])
            for n in range(cols // 256):
                block = slice(n * 256, n * 256 + 256)
                r = jnp.dot(xs, w[:, block], preferred_element_type=F32).astype(BF16)
                p[m, a, :, :, block] = r.reshape(4, 64, 256)

        @pl.when(j == 0)
        def _():
            @pl.loop(0, 4)
            def _(k):
                for m in range(2):
                    for s in range(2):
                        stage1(m, s, 0, k).start()

        @pl.when((j == 1) | (j == 2))
        def _():
            @pl.loop(0, 4)
            def _(k):
                for m in range(2):
                    stage1(m, j - 1, 1, k).start()

    each(4, chunk)

    def add(dst, *refs):
        def group(i):
            r = pl.ds(pl.multiple_of(i * 16, 16), 16)
            v = dst[r, :].astype(F32)
            for ref in refs:
                v = v + ref[r, :].astype(F32)
            dst[r, :] = v.astype(BF16)

        each(dst.shape[0] // 16, group)

    def relay(k):
        for m in range(2):
            for s in range(2):
                stage1(m, s, 0, k).wait_recv()
                b = (second[m] + order_of(k)) % 4
                add(p.at[m, (first[m] + 1 + 2 * s) % 4, b, rows(s)], r1.at[m, s, b])
                stage1(m, s, 2, k).start()

    each(4, relay)

    def settle(m, k):
        b = (second[m] + order_of(k)) % 4
        for s in range(2):
            stage1(m, s, 1, k).wait_recv()
            stage1(m, s, 2, k).wait_recv()
        add(p.at[m, first[m], b], r2.at[m, 0, b], r2.at[m, 1, b])

    for m in range(2):
        settle(m, 0)
        for s in range(2):
            stage2(m, s, 0).start()
    for s in range(2):
        for m in range(2):
            settle(m, 1 + s)
            stage2(m, s, 1).start()
    for s in range(2):
        for m in range(2):
            stage2(m, s, 0).wait_recv()
            add(p.at[m, first[m], (second[m] + 1 + 2 * s) % 4, rows(s)], t1.at[m, s])
            stage2(m, s, 2).start()
    for m in range(2):
        settle(m, 3)
    for m in range(2):
        for s in range(2):
            stage2(m, s, 1).wait_recv()
            stage2(m, s, 2).wait_recv()

    def gated(i):
        r = pl.ds(pl.multiple_of(i * 16, 16), 16)
        g, u = (
            p[m, first[m], second[m], r, :].astype(F32) + t2[m, 0, r, :].astype(F32) + t2[m, 1, r, :].astype(F32)
            for m in range(2)
        )
        g, u = g * sg[...], u * su[...]
        hid[r, :] = g / (1.0 + jnp.exp(-g)) * u

    each(4, gated)
    coef = hartley_entries(FACTOR) / math.sqrt(2048)

    def factor(i):
        r = pl.ds(pl.multiple_of(i * 16, 16), 16)
        blocks = [hid[r, a * 256 : a * 256 + 256] for a in range(FACTOR)]
        for b in range(FACTOR):
            v = blocks[0] * float(coef[b, 0])
            for a in range(1, FACTOR):
                v = v + blocks[a] * float(coef[b, a])
            mid[b, r, :] = v.astype(BF16)

    each(4, factor)
    for b in range(FACTOR):
        out[:, b * 256 : b * 256 + 256] = jnp.dot(mid[b], signs[...], preferred_element_type=F32).astype(BF16)

    for c in g_sends:
        c.wait_send()

    @pl.loop(0, 4)
    def _(k):
        for m in range(2):
            for s in range(2):
                for kind in range(3):
                    stage1(m, s, kind, k).wait_send()

    for m in range(2):
        for s in range(2):
            for kind in range(3):
                stage2(m, s, kind).wait_send()


def gate_up(tokens, gate_codes, up_codes, gate_scale, up_scale):
    width, cols = gate_codes.shape
    vmem = pl.BlockSpec(memory_space=pltpu.VMEM)
    hbm = pl.BlockSpec(memory_space=pl.ANY)
    dma = pltpu.SemaphoreType.DMA
    return pl.pallas_call(
        first_kernel,
        out_shape=jax.ShapeDtypeStruct((64, cols), BF16),
        in_specs=[hbm, hbm, hbm, vmem, vmem, vmem],
        out_specs=vmem,
        scratch_shapes=[
            pltpu.VMEM((4, 4, 64, width), BF16),
            pltpu.VMEM((width, cols), BF16),
            pltpu.VMEM((width, cols), BF16),
            pltpu.VMEM((2, 4, 4, 64, cols), BF16),
            pltpu.VMEM((2, 2, 4, 32, cols), BF16),
            pltpu.VMEM((2, 2, 4, 64, cols), BF16),
            pltpu.VMEM((2, 2, 32, cols), BF16),
            pltpu.VMEM((2, 2, 64, cols), BF16),
            pltpu.VMEM((64, cols), F32),
            pltpu.VMEM((FACTOR, 64, 256), BF16),
            dma((3,)), dma((9,)), dma((9,)),
            dma((2, 2, 3, 4)), dma((2, 2, 3, 4)), dma((2, 2, 3)), dma((2, 2, 3)),
        ],
        compiler_params=pltpu.CompilerParams(
            collective_id=0, has_side_effects=True, vmem_limit_bytes=60 * 1024 * 1024
        ),
        name="gate_up_sum",
    )(
        tokens.reshape(2, 64, width), gate_codes, up_codes,
        gate_scale.reshape(1, cols), up_scale.reshape(1, cols), jnp.asarray(sylvester_signs(256), BF16),
    )


def dequant(codes, scale):
    return (codes.astype(jnp.float32) * scale).astype(jnp.bfloat16)


def cross_rotate(values):
    n_tensor = lax.axis_size("tensor")
    rows_here, columns = values.shape
    signs = jnp.asarray(sylvester_signs(n_tensor), F32)
    mixed_vals = jnp.einsum(
        "rtc,st->rsc",
        lax.all_to_all(
            values.reshape(rows_here, 1, columns), "tensor", split_axis=0, concat_axis=1, tiled=True,
        ).astype(jnp.float32),
        signs,
        precision=lax.Precision.HIGHEST,
    )
    outcome = lax.all_to_all(mixed_vals.astype(BF16), "tensor", split_axis=1, concat_axis=0, tiled=True)
    return outcome.reshape(rows_here, columns)


def expanded_rows(shrunk_rows, selected_adapter_index, adapter_expand_weight):
    selected_rows = jnp.take(adapter_expand_weight, selected_adapter_index, axis=0)
    return jnp.einsum(
        "rk,rkd->rd", shrunk_rows, selected_rows.astype(jnp.float32), precision=lax.Precision.HIGHEST,
    )


def body(
    tokens, gate_int_codes, up_int_codes, down_int_codes, gate_column_scale, up_column_scale, down_column_scale,
    row_adapter_index, adapter_shrink_weight, adapter_expand_weight,
):
    total_rows = row_adapter_index.shape[0]
    hidden_columns = gate_int_codes.shape[1]
    model_cols = down_int_codes.shape[1]
    present_adapters = adapter_shrink_weight.shape[0]
    down_w = dequant(down_int_codes, down_column_scale)
    adapter_columns = jnp.transpose(adapter_shrink_weight, (1, 0, 2)).reshape(
        hidden_columns, present_adapters * ADAPTER_RANK
    )
    joint_w = jnp.concatenate([down_w, adapter_columns], axis=1)
    local = gate_up(tokens, gate_int_codes, up_int_codes, gate_column_scale, up_column_scale)
    rotated = cross_rotate(local)
    joint = jnp.dot(
        lax.all_gather(rotated, "dp", axis=0, tiled=True), joint_w, preferred_element_type=jnp.float32,
    )
    base = joint[:, :model_cols]
    shrink_parts = joint[:, model_cols:].reshape(total_rows, present_adapters, ADAPTER_RANK)
    local_ids = row_adapter_index - lax.axis_index("dp") * present_adapters
    owned = (local_ids[:, None] == jnp.arange(present_adapters, dtype=jnp.int32)[None, :]).astype(jnp.float32)
    partial_shrink = jnp.sum(owned[:, :, None] * shrink_parts, axis=1)
    shrunk_rows = lax.psum(partial_shrink, ("dp", "tensor"))
    reduced_sum = lax.psum_scatter(
        base.astype(jnp.bfloat16), "tensor", scatter_dimension=0, tiled=True
    ).astype(jnp.float32)
    rows_mine = reduced_sum.shape[0]
    first_row = lax.axis_index("tensor") * rows_mine
    owned_shrunk_rows = lax.dynamic_slice_in_dim(shrunk_rows, first_row, rows_mine, 0)
    owned_adapter_index = lax.dynamic_slice_in_dim(row_adapter_index, first_row, rows_mine, 0)
    reduced_sum = reduced_sum + expanded_rows(owned_shrunk_rows, owned_adapter_index, adapter_expand_weight)
    return reduced_sum.astype(jnp.bfloat16)


def solution(mesh):
    return jax.shard_map(
        body,
        mesh=mesh,
        in_specs=(
            P("tensor", "dp"), P("dp", "tensor"), P("dp", "tensor"), P("tensor", "dp"), P("tensor"), P("tensor"),
            P("dp"), P(), P("dp", "tensor", None), P(None, None, "dp"),
        ),
        out_specs=P("tensor", "dp"),
        check_vma=False,
    )
```

```python
import math

import jax
import jax.numpy as jnp
import numpy as np
from jax import lax
from jax.experimental import pallas as pl
from jax.experimental.pallas import tpu as pltpu
from jax.sharding import PartitionSpec as P

FACTOR = 13
ADAPTER_RANK = 16
MESH = pl.DeviceIdType.MESH
F32, BF16 = jnp.float32, jnp.bfloat16


def sylvester_signs(order):
    i = np.arange(order)
    common = i[:, None] & i[None, :]
    parity = np.zeros_like(common)
    while common.any():
        parity ^= common & 1
        common = common >> 1
    return 1 - 2 * parity


def hartley_entries(order):
    i = np.arange(order)
    angle = 2.0 * np.pi * ((i[:, None] * i[None, :]) % order) / order
    return (np.cos(angle) + np.sin(angle)) / math.sqrt(order)


def order_of(j):
    return (2 - j + (j // 2) * (7 - 2 * j)) % 4


BATCHES = 2
BATCH_ROWS = 64 // BATCHES
HALF_ROWS = BATCH_ROWS // 2
PART_SPLIT = 8 // (BATCH_ROWS // 16)
PART_COLS = {2: 1664, 4: 896}[PART_SPLIT]


def part_place(t):
    j = t % PART_SPLIT
    first = 1664 * j if PART_SPLIT == 2 else 128 * (6 * j + (j + 2) // 3)
    return t // PART_SPLIT, first


def each(count, do):
    lax.fori_loop(0, count, lambda i, carry: (do(i), carry)[1], 0)


def layer_kernel(
    tok, wg_hbm, wu_hbm, wd_hbm, shrink_hbm, expand_hbm, sg, su, sd, ids, out,
    xb, wg, wu, p, r1, r2, t1, t2, hid, mid, loc, am, bm, cm, rot, wd, ws, we, bs, bsr, sp, spr, spz, spy,
    load_sem, gs, gr, s1s, s1r, s2s, s2r, a_s, a_r, c_s, c_r, g1s, g1r, g2s, g2r, b_s, b_r, h_s, h_r, d_s, d_r,
):
    dp, tensor = lax.axis_index("dp"), lax.axis_index("tensor")
    z, y = dp // 4, dp % 4
    x, core = tensor // 2, tensor % 2
    cols = wg.shape[1]

    def at_x(step, c):
        return (dp, ((x + step) % 4) * 2 + c)

    def at_z(step):
        return (((z + step) % 4) * 4 + y, tensor)

    def at_y(step):
        return (z * 4 + (y + step) % 4, tensor)

    def peer(i):
        return ((x + i // 2) % 4) * 2 + (core + i % 2) % 2

    def before(i):
        return ((x + 4 - i // 2) % 4) * 2 + (core + i % 2) % 2

    far_first = (4, 5, 2, 3, 6, 7, 1)

    loads = [
        pltpu.make_async_copy(tok.at[q, h], xb.at[x, 2 * core + h, pl.ds(32 * q, 32)], load_sem.at[2 * q + h])
        for q in range(2)
        for h in range(2)
    ]
    loads += [
        pltpu.make_async_copy(a, b, load_sem.at[4 + i])
        for i, (a, b) in enumerate(((wg_hbm, wg), (wu_hbm, wu), (wd_hbm, wd), (shrink_hbm, ws), (expand_hbm, we)))
    ]
    for load in loads[:6]:
        load.start()

    near = [at_x(i // 2, (core + i % 2) % 2) for i in range(1, 8)]
    near += [at_z(i) for i in (1, 2, 3)] + [at_y(i) for i in (1, 2, 3)]
    barrier = pltpu.get_barrier_semaphore()
    for who in near:
        pl.semaphore_signal(barrier, inc=1, device_id=who, device_id_type=MESH)
    pl.semaphore_wait(barrier, len(near))

    def remote(src, dst, send, recv, who):
        return pltpu.make_async_remote_copy(
            src_ref=src, dst_ref=dst, send_sem=send, recv_sem=recv, device_id=who, device_id_type=MESH
        )

    def shard(step, c):
        return xb.at[(x + step) % 4, pl.ds(2 * c, 2)]

    def part(step, c, h):
        return xb.at[(x + step) % 4, 2 * c + h]

    mate = at_x(0, 1 - core)
    sent = []

    def launch(copy):
        copy.start()
        sent.append(copy)

    def gather_copy(i, ref, who):
        return remote(ref, ref, gs.at[i], gr.at[i], who)

    def landed(i, ref):
        gather_copy(i, ref, mate).wait_recv()

    def pass_on(i, ref, who):
        launch(gather_copy(i, ref, who))

    for load in loads[:4]:
        load.wait()
    pass_on(1, shard(0, core), at_x(1, core))
    pass_on(2, shard(0, core), at_x(3, core))
    pass_on(0, shard(0, core), mate)
    landed(1, shard(3, core))
    pass_on(3, part(3, core, 0), at_x(1, core))
    pass_on(5, shard(3, core), mate)
    landed(2, shard(1, core))
    pass_on(4, part(1, core, 1), at_x(3, core))
    pass_on(6, shard(1, core), mate)
    landed(3, part(2, core, 0))
    pass_on(7, part(2, core, 0), mate)
    landed(4, part(2, core, 1))
    pass_on(8, part(2, core, 1), mate)
    for load in loads[4:6]:
        load.wait()
    landed(0, shard(0, 1 - core))
    landed(5, shard(3, 1 - core))
    landed(6, shard(1, 1 - core))
    landed(7, part(2, 1 - core, 0))
    landed(8, part(2, 1 - core, 1))

    first, second = (z, y), (y, z)
    along = ((at_z, at_y), (at_y, at_z))

    def rows(q, h):
        return pl.ds(pl.multiple_of(BATCH_ROWS * q + HALF_ROWS * h, HALF_ROWS), HALF_ROWS)

    def batch_rows(q):
        return pl.ds(BATCH_ROWS * q, BATCH_ROWS)

    def half_rows(q):
        return pl.ds(HALF_ROWS * q, HALF_ROWS)

    def stage1(q, m, s, kind, k):
        step = 1 + 2 * s
        b = (second[m] + order_of(k)) % 4
        a = (first[m] + (2 if kind == 0 else step)) % 4
        h = 1 - s if kind == 1 else s
        src = p.at[m, a, b, rows(q, h)]
        dst = r1.at[m, s, b, half_rows(q)] if kind == 0 else r2.at[m, s, b, rows(q, h)]
        i = (q, m, s, kind, k)
        return remote(src, dst, s1s.at[i], s1r.at[i], along[m][0](step))

    def stage2(q, m, s, kind):
        step = 1 + 2 * s
        b = (second[m] + (2 if kind == 0 else step)) % 4
        h = 1 - s if kind == 1 else s
        src = p.at[m, first[m], b, rows(q, h)]
        dst = t1.at[m, s, half_rows(q)] if kind == 0 else t2.at[m, s, rows(q, h)]
        i = (q, m, s, kind)
        return remote(src, dst, s2s.at[i], s2r.at[i], along[m][1](step))

    def send_far(q):
        @pl.loop(0, 4)
        def _(k):
            for m in range(2):
                for s in range(2):
                    stage1(q, m, s, 0, k).start()

    def send_near(q, s):
        @pl.loop(0, 4)
        def _(k):
            for m in range(2):
                stage1(q, m, s, 1, k).start()

    def chunk(j):
        for m, w in ((0, wg), (1, wu)):
            a = (first[m] + order_of(j)) % 4
            xs = (xb[a] if m == 0 else xb[:, a]).reshape(256, xb.shape[-1])
            for n in range(cols // 256):
                block = slice(n * 256, n * 256 + 256)
                r = jnp.dot(xs, w[:, block], preferred_element_type=F32).astype(BF16)
                p[m, a, :, :, block] = r.reshape(4, 64, 256)

        @pl.when(j == 0)
        def _():
            send_far(0)

        @pl.when((j == 1) | (j == 2))
        def _():
            send_near(0, j - 1)

    def add(dst, *refs):
        def group(i):
            r = pl.ds(pl.multiple_of(i * 16, 16), 16)
            v = dst[r, :].astype(F32)
            for ref in refs:
                v = v + ref[r, :].astype(F32)
            dst[r, :] = v.astype(BF16)

        each(dst.shape[0] // 16, group)

    def relay(q):
        def one(k):
            for m in range(2):
                for s in range(2):
                    stage1(q, m, s, 0, k).wait_recv()
                    b = (second[m] + order_of(k)) % 4
                    add(p.at[m, (first[m] + 1 + 2 * s) % 4, b, rows(q, s)], r1.at[m, s, b, half_rows(q)])
                    stage1(q, m, s, 2, k).start()

        each(4, one)

    def settle(q, m, k):
        b = (second[m] + order_of(k)) % 4
        for s in range(2):
            stage1(q, m, s, 1, k).wait_recv()
            stage1(q, m, s, 2, k).wait_recv()
        r = batch_rows(q)
        add(p.at[m, first[m], b, r], r2.at[m, 0, b, r], r2.at[m, 1, b, r])

    def cross_far(q):
        for m in range(2):
            settle(q, m, 0)
            for s in range(2):
                stage2(q, m, s, 0).start()

    def cross_near(q):
        for s in range(2):
            for m in range(2):
                settle(q, m, 1 + s)
                stage2(q, m, s, 1).start()

    def cross_relay(q):
        for s in range(2):
            for m in range(2):
                stage2(q, m, s, 0).wait_recv()
                b = (second[m] + 1 + 2 * s) % 4
                add(p.at[m, first[m], b, rows(q, s)], t1.at[m, s, half_rows(q)])
                stage2(q, m, s, 2).start()

    def cross_end(q):
        for m in range(2):
            settle(q, m, 3)
        for m in range(2):
            for s in range(2):
                stage2(q, m, s, 1).wait_recv()
                stage2(q, m, s, 2).wait_recv()

    coef = hartley_entries(FACTOR) / math.sqrt(2048)
    lanes = lax.broadcasted_iota(jnp.int32, (256, 256), 0) & lax.broadcasted_iota(jnp.int32, (256, 256), 1)
    for shift in (4, 2, 1):
        lanes = lanes ^ (lanes >> shift)
    signs = (1 - 2 * (lanes & 1)).astype(F32).astype(BF16)

    def local_part(q):
        def gated(i):
            r = pl.ds(pl.multiple_of(BATCH_ROWS * q + i * 16, 16), 16)
            g, u = (
                p[m, first[m], second[m], r, :].astype(F32) + t2[m, 0, r, :].astype(F32) + t2[m, 1, r, :].astype(F32)
                for m in range(2)
            )
            g, u = g * sg[...], u * su[...]
            hid[r, :] = g / (1.0 + jnp.exp(-g)) * u

        each(BATCH_ROWS // 16, gated)

        def factor(i):
            r = pl.ds(pl.multiple_of(BATCH_ROWS * q + i * 16, 16), 16)
            blocks = [hid[r, a * 256 : a * 256 + 256] for a in range(FACTOR)]
            for b in range(FACTOR):
                v = blocks[0] * float(coef[b, 0])
                for a in range(1, FACTOR):
                    v = v + blocks[a] * float(coef[b, a])
                mid[b, r, :] = v.astype(BF16)

        each(BATCH_ROWS // 16, factor)
        r = batch_rows(q)
        turned = jnp.dot(
            mid[:, r, :].reshape(FACTOR * BATCH_ROWS, 256), signs, preferred_element_type=F32
        ).astype(BF16)
        for b in range(FACTOR):
            loc[r, b * 256 : b * 256 + 256] = turned[b * BATCH_ROWS : (b + 1) * BATCH_ROWS]
        for i in far_first:
            launch(mix_copy(q, i))
        am[q, tensor] = my_part(q, tensor)[...]

    def my_part(q, t):
        group, start = part_place(t)
        r = pl.ds(pl.multiple_of(BATCH_ROWS * q + 16 * group, 16), 16)
        return loc.at[r, pl.ds(pl.multiple_of(start, 128), PART_COLS)]

    def mix_copy(q, i):
        to = peer(i)
        return remote(my_part(q, to), am.at[q, tensor], a_s.at[q, i], a_r.at[q, i], (dp, to))

    def back_copy(q, i):
        to = peer(i)
        return remote(bm.at[q, to], cm.at[q, tensor], c_s.at[q, i], c_r.at[q, i], (dp, to))

    def mix(q):
        for i in far_first:
            mix_copy(q, i).wait_recv()
        for c in range(PART_COLS // 128):
            lane = slice(c * 128, c * 128 + 128)
            v = [am[q, t, :, lane].astype(F32) for t in range(8)]
            for bit in (1, 2, 4):
                v = [v[t] + v[t ^ bit] if t & bit == 0 else v[t ^ bit] - v[t] for t in range(8)]
            for t in range(8):
                bm[q, t, :, lane] = v[t].astype(BF16)
        for i in far_first:
            launch(back_copy(q, i))
        cm[q, tensor] = bm[q, tensor]

    def off(c):
        return c + (c // 2) * (5 - 2 * c)

    def held(q, f, c1, c2):
        c = (c1 % 4, c2 % 4) if f == 0 else (c2 % 4, c1 % 4)
        return rot.at[c[0], c[1], rows(q, f)]

    def half_cols(s):
        return pl.ds(s * (cols // 2), cols // 2)

    def spread1(q, f, s, kind):
        step = 1 + 2 * s
        ref = held(q, f, first[f] + (0 if kind == 0 else 4 - step), second[f])
        if kind == 1:
            ref = ref.at[:, half_cols(s)]
        i = (q, f, s, kind)
        return remote(ref, ref, g1s.at[i], g1r.at[i], along[f][0](step))

    def spread2(q, f, s, kind, c):
        step = 1 + 2 * s
        ref = held(q, f, first[f] + off(c), second[f] + (0 if kind == 0 else 4 - step))
        if kind == 1:
            ref = ref.at[:, half_cols(s)]
        i = (q, f, s, kind, c)
        return remote(ref, ref, g2s.at[i], g2r.at[i], along[f][1](step))

    def got1(q, f, s, kind):
        step = 1 + 2 * s
        ref = held(q, f, first[f] + (4 - step if kind == 0 else 2), second[f])
        if kind == 1:
            ref = ref.at[:, half_cols(s)]
        i = (q, f, s, kind)
        remote(ref, ref, g1s.at[i], g1r.at[i], along[f][0](step)).wait_recv()

    def got2(q, f, s, kind, c):
        step = 1 + 2 * s
        ref = held(q, f, first[f] + off(c), second[f] + (4 - step if kind == 0 else 2))
        if kind == 1:
            ref = ref.at[:, half_cols(s)]
        i = (q, f, s, kind, c)
        remote(ref, ref, g2s.at[i], g2r.at[i], along[f][1](step)).wait_recv()

    def spread_start(q):
        for i in far_first:
            back_copy(q, i).wait_recv()
        for t in range(8):
            group, start = part_place(t)
            r = pl.ds(BATCH_ROWS * q + 16 * group, 16)
            rot[z, y, r, start : start + PART_COLS] = cm[q, t]
        for f in range(2):
            for s in range(2):
                launch(spread1(q, f, s, 0))
        for f in range(2):
            for s in range(2):
                launch(spread2(q, f, s, 0, 0))

    def spread_mid(q):
        for s in range(2):
            for f in range(2):
                got1(q, f, s, 0)
                launch(spread1(q, f, s, 1))
        for s in range(2):
            for f in range(2):
                for s2 in range(2):
                    launch(spread2(q, f, s2, 0, 2 - s))

    def spread_far(q):
        for f in range(2):
            for s in range(2):
                got1(q, f, s, 1)
            for s2 in range(2):
                launch(spread2(q, f, s2, 0, 3))

    def spread_relay(q, c):
        for f in range(2):
            for s in range(2):
                got2(q, f, s, 0, c)
                launch(spread2(q, f, s, 1, c))

    def spread_end(q):
        for c in range(4):
            for f in range(2):
                for s in range(2):
                    got2(q, f, s, 1, c)

    def sum_copy(q, i):
        to = peer(i)
        return remote(bs.at[q, to], bsr.at[q, tensor], b_s.at[q, i], b_r.at[q, i], (dp, to))

    def down(q):
        def group(g):
            lhs = rot[pl.ds(2 * g, 2), :, batch_rows(q), :].reshape(8 * BATCH_ROWS, cols)
            base = jnp.dot(lhs, wd[...], preferred_element_type=F32).astype(BF16)
            bs[q, pl.ds(4 * g, 4)] = base.reshape(4, 2 * BATCH_ROWS, base.shape[-1])
            parts = lax.dot_general(ws[...], lhs, (((1,), (1,)), ((), ())), preferred_element_type=F32)
            id_row = ids[q, g]
            total = jnp.zeros((ADAPTER_RANK, 8 * BATCH_ROWS), F32)
            for a in range(16):
                mine = id_row == dp * 16 + a
                total = total + jnp.where(mine, parts[a * 16 : a * 16 + 16], 0.0)
            lane = lax.broadcasted_iota(jnp.int32, (ADAPTER_RANK, 128), 1)
            for i in range(2):
                v = total[:, i * 128 : i * 128 + 128]
                turned = pltpu.roll(v, 64, 1)
                even, odd = 4 * g + 2 * i, 4 * g + 2 * i + 1
                if q == 0:
                    sp[even] = v
                    sp[odd] = turned
                else:
                    sp[even] = jnp.where(lane < 64, sp[even], turned)
                    sp[odd] = jnp.where(lane < 64, sp[odd], v)

        each(2, group)
        for i in far_first:
            launch(sum_copy(q, i))

    def shrink_copy(i):
        to = peer(i)
        return remote(sp.at[to], spr.at[tensor], h_s.at[i], h_r.at[i], (dp, to))

    def shrink_z(i):
        return remote(spz.at[z], spz.at[z], d_s.at[0, i], d_r.at[0, i], at_z(i))

    def shrink_y(i):
        return remote(spy.at[y], spy.at[y], d_s.at[1, i], d_r.at[1, i], at_y(i))

    def total(refs):
        v = refs[0]
        for ref in refs[1:]:
            v = v + ref
        return v

    def finish():
        for i in far_first:
            launch(shrink_copy(i))
        for i in far_first:
            shrink_copy(i).wait_recv()
        spr[tensor] = sp[tensor]
        spz[z] = total([spr[t] for t in range(8)])
        for i in (2, 1, 3):
            launch(shrink_z(i))
        for i in (2, 1, 3):
            shrink_z(i).wait_recv()
        spy[y] = total([spz[c] for c in range(4)])
        for i in (2, 1, 3):
            launch(shrink_y(i))
        for q in range(BATCHES):
            for i in far_first:
                sum_copy(q, i).wait_recv()
            bsr[q, tensor] = bs[q, tensor]
        for i in (2, 1, 3):
            shrink_y(i).wait_recv()
        shrunk = total([spy[c] for c in range(4)])
        wide = jnp.concatenate([shrunk] * 8, axis=0).T
        own_ids = jnp.broadcast_to(ids[2, tensor, :, :128], (128, 128)).astype(F32).T
        lane_adapter = (lax.broadcasted_iota(jnp.int32, (128, 128), 1) // ADAPTER_RANK).astype(F32)
        spot = own_ids - lane_adapter
        chosen = jnp.concatenate(
            [jnp.where(spot == float(8 * j), wide, 0.0).astype(BF16) for j in range(32)], axis=1
        )
        extra = jnp.dot(chosen, we[...], preferred_element_type=F32)
        for q in range(BATCHES):
            r = slice(2 * BATCH_ROWS * q, 2 * BATCH_ROWS * (q + 1))
            base = total([bsr[q, t].astype(F32) for t in range(8)])
            out[r, :] = (base * sd[...] + extra[r]).astype(BF16)

    each(4, chunk)
    for load in loads[6:]:
        load.start()
    relay(0)
    send_far(1)
    send_near(1, 0)
    send_near(1, 1)
    cross_far(0)
    cross_near(0)
    cross_relay(0)
    relay(1)
    cross_end(0)
    local_part(0)
    cross_far(1)
    mix(0)
    cross_near(1)
    spread_start(0)
    cross_relay(1)
    spread_mid(0)
    cross_end(1)
    local_part(1)
    spread_far(0)
    mix(1)
    for c in range(2):
        spread_relay(0, c)
    spread_start(1)
    for c in range(2, 4):
        spread_relay(0, c)
    spread_mid(1)
    for load in loads[6:]:
        load.wait()
    spread_end(0)
    spread_far(1)
    down(0)
    for c in range(4):
        spread_relay(1, c)
    spread_end(1)
    down(1)
    finish()

    for copy in sent:
        copy.wait_send()

    @pl.loop(0, 4)
    def _(k):
        for q in range(BATCHES):
            for m in range(2):
                for s in range(2):
                    for kind in range(3):
                        stage1(q, m, s, kind, k).wait_send()

    for q in range(BATCHES):
        for m in range(2):
            for s in range(2):
                for kind in range(3):
                    stage2(q, m, s, kind).wait_send()


def body(
    tokens, gate_int_codes, up_int_codes, down_int_codes, gate_column_scale, up_column_scale, down_column_scale,
    row_adapter_index, adapter_shrink_weight, adapter_expand_weight,
):
    rows, width = tokens.shape
    cols, wide = down_int_codes.shape
    shrink = jnp.transpose(adapter_shrink_weight, (0, 2, 1)).reshape(-1, cols)
    expand = adapter_expand_weight.reshape(-1, wide)
    by_batch = row_adapter_index.reshape(2, 4, 2, 64).transpose(2, 0, 1, 3).reshape(2, 2, 256)
    by_batch = jnp.pad(by_batch, ((0, 0), (0, 6), (0, 0)))
    by_owner = jnp.pad(row_adapter_index.reshape(8, 128), ((0, 0), (0, 128)))
    ids = jnp.concatenate([by_batch, by_owner[None]], axis=0)[:, :, None, :]
    vmem = pl.BlockSpec(memory_space=pltpu.VMEM)
    hbm = pl.BlockSpec(memory_space=pl.ANY)

    def dma(*shape):
        return [pltpu.SemaphoreType.DMA(shape)] * 2

    n = BATCHES
    return pl.pallas_call(
        layer_kernel,
        out_shape=jax.ShapeDtypeStruct((rows, wide), BF16),
        in_specs=[hbm] * 6 + [vmem] * 4,
        out_specs=vmem,
        scratch_shapes=[
            pltpu.VMEM((4, 4, 64, width), BF16),
            pltpu.VMEM((width, cols), BF16),
            pltpu.VMEM((width, cols), BF16),
            pltpu.VMEM((2, 4, 4, 64, cols), BF16),
            pltpu.VMEM((2, 2, 4, 32, cols), BF16),
            pltpu.VMEM((2, 2, 4, 64, cols), BF16),
            pltpu.VMEM((2, 2, 32, cols), BF16),
            pltpu.VMEM((2, 2, 64, cols), BF16),
            pltpu.VMEM((64, cols), F32),
            pltpu.VMEM((FACTOR, 64, 256), BF16),
            pltpu.VMEM((64, cols), BF16),
            pltpu.VMEM((n, 8, 16, PART_COLS), BF16),
            pltpu.VMEM((n, 8, 16, PART_COLS), BF16),
            pltpu.VMEM((n, 8, 16, PART_COLS), BF16),
            pltpu.VMEM((4, 4, 64, cols), BF16),
            pltpu.VMEM((cols, wide), BF16),
            pltpu.VMEM((16 * ADAPTER_RANK, cols), BF16),
            pltpu.VMEM((256 * ADAPTER_RANK, wide), BF16),
            pltpu.VMEM((n, 8, 2 * BATCH_ROWS, wide), BF16),
            pltpu.VMEM((n, 8, 2 * BATCH_ROWS, wide), BF16),
            pltpu.VMEM((8, ADAPTER_RANK, 128), F32),
            pltpu.VMEM((8, ADAPTER_RANK, 128), F32),
            pltpu.VMEM((4, ADAPTER_RANK, 128), F32),
            pltpu.VMEM((4, ADAPTER_RANK, 128), F32),
            pltpu.SemaphoreType.DMA((9,)),
            *dma(9), *dma(n, 2, 2, 3, 4), *dma(n, 2, 2, 3), *dma(n, 8), *dma(n, 8),
            *dma(n, 2, 2, 2), *dma(n, 2, 2, 2, 4), *dma(n, 8), *dma(8), *dma(2, 4),
        ],
        compiler_params=pltpu.CompilerParams(
            collective_id=0, has_side_effects=True, vmem_limit_bytes=63 * 1024 * 1024
        ),
        name="layer",
    )(
        tokens.reshape(2, 2, 32, width), gate_int_codes, up_int_codes, down_int_codes, shrink, expand,
        gate_column_scale.reshape(1, cols), up_column_scale.reshape(1, cols), down_column_scale.reshape(1, wide), ids,
    )


def solution(mesh):
    return jax.shard_map(
        body,
        mesh=mesh,
        in_specs=(
            P("tensor", "dp"), P("dp", "tensor"), P("dp", "tensor"), P("tensor", "dp"), P("tensor"), P("tensor"),
            P("dp"), P(), P("dp", "tensor", None), P(None, None, "dp"),
        ),
        out_specs=P("tensor", "dp"),
        check_vma=False,
    )
```

```python
import math

import jax
import jax.numpy as jnp
import numpy as np
from jax import lax
from jax.experimental import pallas as pl
from jax.experimental.pallas import tpu as pltpu
from jax.sharding import PartitionSpec as P

FACTOR = 13
ADAPTER_RANK = 16
MESH = pl.DeviceIdType.MESH
F32, BF16 = jnp.float32, jnp.bfloat16


def sylvester_signs(order):
    i = np.arange(order)
    common = i[:, None] & i[None, :]
    parity = np.zeros_like(common)
    while common.any():
        parity ^= common & 1
        common = common >> 1
    return 1 - 2 * parity


def hartley_entries(order):
    i = np.arange(order)
    angle = 2.0 * np.pi * ((i[:, None] * i[None, :]) % order) / order
    return (np.cos(angle) + np.sin(angle)) / math.sqrt(order)


def order_of(j):
    return (2 - j + (j // 2) * (7 - 2 * j)) % 4


BATCHES = 2
BATCH_ROWS = 64 // BATCHES
HALF_ROWS = BATCH_ROWS // 2
PART_SPLIT = 8 // (BATCH_ROWS // 16)
PART_COLS = {2: 1664, 4: 896}[PART_SPLIT]


def part_place(t):
    j = t % PART_SPLIT
    first = 1664 * j if PART_SPLIT == 2 else 128 * (6 * j + (j + 2) // 3)
    return t // PART_SPLIT, first


def each(count, do):
    lax.fori_loop(0, count, lambda i, carry: (do(i), carry)[1], 0)


def layer_kernel(
    tok, wg_hbm, wu_hbm, wd_hbm, shrink_hbm, expand_hbm, sg_hbm, su_hbm, sd_hbm, ids_hbm, out,
    sgv, suv, sdv, ids, scales, xb, wg, wu, p, r1, r2, t1, t2, hid, mid, loc, am, bm, cm, rot, wd, ws, we, bs, bsr, sp, spr, spd,
    load_sem, send_sem, gr, far_r, near_r, t1_r, t2_r, a_r, c_r, g1_r, g1x_r, g2_r, g2x_r, b_r, h_r, d_r,
):
    dp, tensor = lax.axis_index("dp"), lax.axis_index("tensor")
    z, y = dp // 4, dp % 4
    x, core = tensor // 2, tensor % 2
    cols = wg.shape[1]

    def at_x(step, c):
        return (dp, ((x + step) % 4) * 2 + c)

    def at_z(step):
        return (((z + step) % 4) * 4 + y, tensor)

    def at_y(step):
        return (z * 4 + (y + step) % 4, tensor)

    def peer(i):
        return ((x + i // 2) % 4) * 2 + (core + i % 2) % 2

    def before(i):
        return ((x + 4 - i // 2) % 4) * 2 + (core + i % 2) % 2

    far_first = (4, 5, 2, 3, 6, 7, 1)

    pairs = [(tok.at[q, h], xb.at[x, 2 * core + h, pl.ds(32 * q, 32)]) for q in range(2) for h in range(2)]
    pairs += [(wg_hbm, wg), (wu_hbm, wu), (sg_hbm, sgv), (su_hbm, suv), (sd_hbm, sdv), (ids_hbm, ids)]
    pairs += [(wd_hbm, wd), (shrink_hbm, ws), (expand_hbm, we)]
    loads = [pltpu.make_async_copy(a, b, load_sem.at[i]) for i, (a, b) in enumerate(pairs)]
    for load in loads[:10]:
        load.start()

    near = [at_x(i // 2, (core + i % 2) % 2) for i in range(1, 8)]
    others = [(((z + i // 4) % 4) * 4 + (y + i % 4) % 4, tensor) for i in range(1, 16)]
    near += others
    barrier = pltpu.get_barrier_semaphore()
    for who in near:
        pl.semaphore_signal(barrier, inc=1, device_id=who, device_id_type=MESH)
    pl.semaphore_wait(barrier, len(near))

    def remote(src, dst, send, recv, who):
        return pltpu.make_async_remote_copy(
            src_ref=src, dst_ref=dst, send_sem=send, recv_sem=recv, device_id=who, device_id_type=MESH
        )

    mate = at_x(0, 1 - core)
    def shard(q, step, c):
        return xb.at[(x + step) % 4, pl.ds(2 * c, 2), pl.ds(32 * q, 32)]

    def await_bytes(ref, sem):
        remote(ref, ref, send_sem.at[0], sem, mate).wait_recv()

    def gather_copy(q, i, src, dst, who):
        return remote(src, dst, send_sem.at[0 if 0 < i < 4 else 1], gr.at[q, i % 4 if i < 4 else 0], who)

    def gather_start(q):
        for step in (2, 1, 3):
            gather_copy(q, step, tok.at[q], shard(q, 0, core), at_x(step, core)).start()
        gather_copy(q, 0, tok.at[q], shard(q, 0, core), mate).start()

    def gather_mate(q):
        for step in (1, 3, 2):
            ref = shard(q, 4 - step, core)
            await_bytes(ref, gr.at[q, step])
            gather_copy(q, 4, ref, ref, mate).start()

    def gather_end(q):
        await_bytes(xb.at[0], gr.at[q, 0])

    first, second = (z, y), (y, z)
    along = ((at_z, at_y), (at_y, at_z))

    def rows(q, h):
        return pl.ds(pl.multiple_of(BATCH_ROWS * q + HALF_ROWS * h, HALF_ROWS), HALF_ROWS)

    def batch_rows(q):
        return pl.ds(BATCH_ROWS * q, BATCH_ROWS)

    def half_rows(q):
        return pl.ds(HALF_ROWS * q, HALF_ROWS)

    def stage1(q, m, s, kind, k):
        step = 1 + 2 * s
        b = (second[m] + order_of(k)) % 4
        a = (first[m] + (2 if kind == 0 else step)) % 4
        h = 1 - s if kind == 1 else s
        src = p.at[m, a, b, rows(q, h)]
        dst = r1.at[m, s, b, half_rows(q)] if kind == 0 else r2.at[m, s, b, rows(q, h)]
        sem = far_r.at[q, k] if kind == 0 else near_r.at[q, m, k]
        return remote(src, dst, send_sem.at[2], sem, along[m][0](step))

    def stage2(q, m, s, kind):
        step = 1 + 2 * s
        b = (second[m] + (2 if kind == 0 else step)) % 4
        h = 1 - s if kind == 1 else s
        src = p.at[m, first[m], b, rows(q, h)]
        dst = t1.at[m, s, half_rows(q)] if kind == 0 else t2.at[m, s, rows(q, h)]
        sem = t1_r.at[q, s] if kind == 0 else t2_r.at[q]
        return remote(src, dst, send_sem.at[3], sem, along[m][1](step))

    def send_far(q):
        @pl.loop(0, 4)
        def _(k):
            for m in range(2):
                for s in range(2):
                    stage1(q, m, s, 0, k).start()

    def send_near(q, s):
        @pl.loop(0, 4)
        def _(k):
            for m in range(2):
                stage1(q, m, s, 1, k).start()

    def chunk(q, j):
        for m, w in ((0, wg), (1, wu)):
            a = (first[m] + order_of(j)) % 4
            r = batch_rows(q)
            xs = (xb[a, :, r] if m == 0 else xb[:, a, r]).reshape(4 * BATCH_ROWS, xb.shape[-1])
            for n in range(cols // 256):
                block = slice(n * 256, n * 256 + 256)
                v = jnp.dot(xs, w[:, block], preferred_element_type=F32).astype(BF16)
                p[m, a, :, r, block] = v.reshape(4, BATCH_ROWS, 256)

    def first_batch(j):
        chunk(0, j)

        @pl.when(j == 0)
        def _():
            send_far(0)

        @pl.when((j == 1) | (j == 2))
        def _():
            send_near(0, j - 1)

    def second_batch(j):
        chunk(1, j)

    def spread_scales():
        for i in range(cols // 128):
            for m, ref in enumerate((sgv, suv)):
                scales[m, :, i * 128 : i * 128 + 128] = ref[i : i + 1, :]

    def add(dst, *refs):
        def group(i):
            r = pl.ds(pl.multiple_of(i * 16, 16), 16)
            v = dst[r, :].astype(F32)
            for ref in refs:
                v = v + ref[r, :].astype(F32)
            dst[r, :] = v.astype(BF16)

        each(dst.shape[0] // 16, group)

    def relay(q):
        def one(k):
            await_bytes(r1.at[:, :, 0, half_rows(q)], far_r.at[q, k])
            for m in range(2):
                for s in range(2):
                    b = (second[m] + order_of(k)) % 4
                    add(p.at[m, (first[m] + 1 + 2 * s) % 4, b, rows(q, s)], r1.at[m, s, b, half_rows(q)])
                    stage1(q, m, s, 2, k).start()

        each(4, one)

    def settle(q, m, k):
        b = (second[m] + order_of(k)) % 4
        r = batch_rows(q)
        await_bytes(r2.at[m, :, b, r], near_r.at[q, m, k])
        add(p.at[m, first[m], b, r], r2.at[m, 0, b, r], r2.at[m, 1, b, r])

    def cross_far(q):
        for m in range(2):
            settle(q, m, 0)
            for s in range(2):
                stage2(q, m, s, 0).start()

    def cross_near(q):
        for s in range(2):
            for m in range(2):
                settle(q, m, 1 + s)
                stage2(q, m, s, 1).start()

    def cross_relay(q):
        for s in range(2):
            await_bytes(t1.at[:, s, half_rows(q)], t1_r.at[q, s])
            for m in range(2):
                b = (second[m] + 1 + 2 * s) % 4
                add(p.at[m, first[m], b, rows(q, s)], t1.at[m, s, half_rows(q)])
                stage2(q, m, s, 2).start()

    def cross_end(q):
        for m in range(2):
            settle(q, m, 3)
        await_bytes(t2.at[:, :, batch_rows(q)], t2_r.at[q])

    coef = hartley_entries(FACTOR) / math.sqrt(2048)
    lanes = lax.broadcasted_iota(jnp.int32, (256, 256), 0) & lax.broadcasted_iota(jnp.int32, (256, 256), 1)
    for shift in (4, 2, 1):
        lanes = lanes ^ (lanes >> shift)
    signs = (1 - 2 * (lanes & 1)).astype(F32).astype(BF16)

    def local_part(q):
        def gated(i):
            r = pl.ds(pl.multiple_of(BATCH_ROWS * q + i * 16, 16), 16)
            g, u = (
                p[m, first[m], second[m], r, :].astype(F32) + t2[m, 0, r, :].astype(F32) + t2[m, 1, r, :].astype(F32)
                for m in range(2)
            )
            g, u = g * scales[0], u * scales[1]
            hid[r, :] = g / (1.0 + jnp.exp(-g)) * u

        each(BATCH_ROWS // 16, gated)

        def factor(i):
            r = pl.ds(pl.multiple_of(BATCH_ROWS * q + i * 16, 16), 16)
            blocks = [hid[r, a * 256 : a * 256 + 256] for a in range(FACTOR)]
            for b in range(FACTOR):
                v = blocks[0] * float(coef[b, 0])
                for a in range(1, FACTOR):
                    v = v + blocks[a] * float(coef[b, a])
                mid[b, r, :] = v.astype(BF16)

        each(BATCH_ROWS // 16, factor)
        r = batch_rows(q)
        turned = jnp.dot(
            mid[:, r, :].reshape(FACTOR * BATCH_ROWS, 256), signs, preferred_element_type=F32
        ).astype(BF16)
        for b in range(FACTOR):
            loc[r, b * 256 : b * 256 + 256] = turned[b * BATCH_ROWS : (b + 1) * BATCH_ROWS]
        for i in far_first:
            mix_copy(q, i).start()
        am[q, tensor] = my_part(q, tensor)[...]

    def my_part(q, t):
        group, start = part_place(t)
        r = pl.ds(pl.multiple_of(BATCH_ROWS * q + 16 * group, 16), 16)
        return loc.at[r, pl.ds(pl.multiple_of(start, 128), PART_COLS)]

    def mix_copy(q, i):
        to = peer(i)
        return remote(my_part(q, to), am.at[q, tensor], send_sem.at[4], a_r.at[q], (dp, to))

    def back_copy(q, i):
        to = peer(i)
        return remote(bm.at[q, to], cm.at[q, tensor], send_sem.at[5], c_r.at[q], (dp, to))

    def mix(q):
        await_bytes(am.at[q, pl.ds(0, 7)], a_r.at[q])
        for c in range(PART_COLS // 128):
            lane = slice(c * 128, c * 128 + 128)
            v = [am[q, t, :, lane].astype(F32) for t in range(8)]
            for bit in (1, 2, 4):
                v = [v[t] + v[t ^ bit] if t & bit == 0 else v[t ^ bit] - v[t] for t in range(8)]
            for t in range(8):
                bm[q, t, :, lane] = v[t].astype(BF16)
        for i in far_first:
            back_copy(q, i).start()
        cm[q, tensor] = bm[q, tensor]

    def off(c):
        return c + (c // 2) * (5 - 2 * c)

    def held(q, f, c1, c2):
        c = (c1 % 4, c2 % 4) if f == 0 else (c2 % 4, c1 % 4)
        return rot.at[c[0], c[1], rows(q, f)]

    def half_cols(s):
        return pl.ds(s * (cols // 2), cols // 2)

    def spread1(q, f, s, kind):
        step = 1 + 2 * s
        ref = held(q, f, first[f] + (0 if kind == 0 else 4 - step), second[f])
        if kind == 1:
            ref = ref.at[:, half_cols(s)]
        sem = g1_r.at[q, s] if kind == 0 else g1x_r.at[q]
        return remote(ref, ref, send_sem.at[6], sem, along[f][0](step))

    def spread2(q, f, s, kind, c):
        step = 1 + 2 * s
        ref = held(q, f, first[f] + off(c), second[f] + (0 if kind == 0 else 4 - step))
        if kind == 1:
            ref = ref.at[:, half_cols(s)]
        sem = g2_r.at[q, c] if kind == 0 else g2x_r.at[q, c]
        return remote(ref, ref, send_sem.at[7], sem, along[f][1](step))

    def spread_start(q):
        await_bytes(cm.at[q, pl.ds(0, 7)], c_r.at[q])
        for t in range(8):
            group, start = part_place(t)
            r = pl.ds(BATCH_ROWS * q + 16 * group, 16)
            rot[z, y, r, start : start + PART_COLS] = cm[q, t]
        for f in range(2):
            for s in range(2):
                spread1(q, f, s, 0).start()
        for f in range(2):
            for s in range(2):
                spread2(q, f, s, 0, 0).start()

    def spread_mid(q):
        for s in range(2):
            await_bytes(rot.at[0, 0, batch_rows(q)], g1_r.at[q, s])
            for f in range(2):
                spread1(q, f, s, 1).start()
        for s in range(2):
            for f in range(2):
                for s2 in range(2):
                    spread2(q, f, s2, 0, 2 - s).start()

    def spread_far(q):
        await_bytes(rot.at[0, 0, batch_rows(q)], g1x_r.at[q])
        for f in range(2):
            for s2 in range(2):
                spread2(q, f, s2, 0, 3).start()

    def spread_relay(q, c):
        await_bytes(rot.at[0, 0], g2_r.at[q, c])
        for f in range(2):
            for s in range(2):
                spread2(q, f, s, 1, c).start()

    def spread_end(q):
        for c in range(4):
            await_bytes(rot.at[0, 0, batch_rows(q)], g2x_r.at[q, c])

    def sum_piece(q, c1, c2):
        to = 2 * c1 + c2 // 2
        r = pl.ds(pl.multiple_of(BATCH_ROWS * (c2 % 2), BATCH_ROWS), BATCH_ROWS)
        return remote(bs.at[q, to, r], bsr.at[q, tensor, r], send_sem.at[8], b_r.at[q], (dp, to)), to, r

    def ids_of(t):
        row = ids[0:1, :]
        for i in range(1, 8):
            row = jnp.where(t == i, ids[i : i + 1, :], row)
        return row

    lane = lax.broadcasted_iota(jnp.int32, (ADAPTER_RANK, 128), 1)

    def shrink(q, c):
        lhs = rot[c, :, batch_rows(q), :].reshape(4 * BATCH_ROWS, cols)
        parts = lax.dot_general(ws[...], lhs, (((1,), (1,)), ((), ())), preferred_element_type=F32)
        even, odd = 2 * c, 2 * c + 1
        if q == 0:
            id_row = jnp.where(lane[:1] < 64, ids_of(even), pltpu.roll(ids_of(odd), 64, 1))
        else:
            id_row = jnp.where(lane[:1] < 64, pltpu.roll(ids_of(even), 64, 1), ids_of(odd))
        v = jnp.zeros((ADAPTER_RANK, 128), F32)
        for a in range(16):
            v = v + jnp.where(id_row == dp * 16 + a, parts[a * 16 : a * 16 + 16], 0.0)
        turned = pltpu.roll(v, 64, 1)
        if q == 0:
            sp[even] = v
            sp[odd] = turned
        else:
            sp[even] = jnp.where(lane < 64, sp[even], turned)
            sp[odd] = jnp.where(lane < 64, sp[odd], v)

    def shrink_all(q):
        each(4, lambda c: shrink(q, c))

    def shrink_send():
        for i in far_first:
            shrink_copy(i).start()

    def down(q, places):
        places = [((z + i) % 4, (y + j) % 4) for i, j in places]
        lhs = jnp.concatenate([rot[c1, c2, batch_rows(q)] for c1, c2 in places], axis=0)
        base = jnp.dot(lhs, wd[...], preferred_element_type=F32).astype(BF16)
        for n, (c1, c2) in enumerate(places):
            copy, to, r = sum_piece(q, c1, c2)
            bs[q, to, r] = base[n * BATCH_ROWS : (n + 1) * BATCH_ROWS]

            @pl.when(to != tensor)
            def _():
                copy.start()

    def down_early(q):
        for j in (0, 1, 3):
            down(q, [(i, j) for i in (0, 1, 3)])

    def down_late(q):
        down(q, [(2, j) for j in range(4)])
        down(q, [(i, 2) for i in (0, 1, 3)])

    def shrink_copy(i):
        to = peer(i)
        return remote(sp.at[to], spr.at[tensor], send_sem.at[9], h_r.at[0], (dp, to))

    def shrink_across(who):
        return remote(spd.at[dp], spd.at[dp], send_sem.at[10], d_r.at[0], who)

    def total(refs):
        v = refs[0]
        for ref in refs[1:]:
            v = v + ref
        return v

    def finish():
        await_bytes(spr.at[pl.ds(0, 7)], h_r.at[0])
        spr[tensor] = sp[tensor]
        spd[dp] = total([spr[t] for t in range(8)])
        for who in others:
            shrink_across(who).start()
        for q in range(BATCHES):
            await_bytes(bsr.at[q, pl.ds(0, 7)], b_r.at[q])
            bsr[q, tensor] = bs[q, tensor]
        await_bytes(spd.at[pl.ds(0, 15)], d_r.at[0])
        shrunk = total([spd[c] for c in range(16)])
        wide = jnp.concatenate([shrunk] * 8, axis=0).T
        own_ids = jnp.broadcast_to(ids_of(tensor), (128, 128)).astype(F32).T
        lane_adapter = (lax.broadcasted_iota(jnp.int32, (128, 128), 1) // ADAPTER_RANK).astype(F32)
        spot = own_ids - lane_adapter
        chosen = jnp.concatenate(
            [jnp.where(spot == float(8 * j), wide, 0.0).astype(BF16) for j in range(32)], axis=1
        )
        extra = jnp.dot(chosen, we[...], preferred_element_type=F32)
        for q in range(BATCHES):
            r = slice(2 * BATCH_ROWS * q, 2 * BATCH_ROWS * (q + 1))
            base = total([bsr[q, t].astype(F32) for t in range(8)])
            for i in range(out.shape[1] // 128):
                block = slice(i * 128, i * 128 + 128)
                out[r, block] = (base[:, block] * sdv[i : i + 1, :] + extra[r, block]).astype(BF16)

    gather_start(0)
    gather_mate(0)
    for load in loads[:6]:
        load.wait()
    gather_end(0)
    gather_start(1)
    each(4, first_batch)
    gather_mate(1)
    gather_end(1)
    for load in loads[10:]:
        load.start()
    each(4, second_batch)
    for load in loads[6:10]:
        load.wait()
    spread_scales()
    relay(0)
    send_far(1)
    send_near(1, 0)
    send_near(1, 1)
    cross_far(0)
    cross_near(0)
    cross_relay(0)
    relay(1)
    cross_end(0)
    local_part(0)
    cross_far(1)
    mix(0)
    cross_near(1)
    spread_start(0)
    cross_relay(1)
    spread_mid(0)
    cross_end(1)
    local_part(1)
    spread_far(0)
    mix(1)
    for c in range(2):
        spread_relay(0, c)
    spread_start(1)
    for c in range(2, 4):
        spread_relay(0, c)
    spread_mid(1)
    for load in loads[10:]:
        load.wait()
    spread_end(0)
    spread_far(1)
    shrink_all(0)
    down_early(0)
    down_late(0)
    for c in range(4):
        spread_relay(1, c)
    down_early(1)
    spread_end(1)
    shrink_all(1)
    shrink_send()
    down_late(1)
    finish()

    gone = (
        xb.at[pl.ds(0, 2), pl.ds(0, 3)], xb.at[pl.ds(0, 2)], p.at[:, pl.ds(0, 3)], p.at[0, pl.ds(0, 2), pl.ds(0, 3)],
        am.at[:, pl.ds(0, 7)], cm.at[:, pl.ds(0, 7)], rot.at[0, pl.ds(0, 3)], rot.at[pl.ds(0, 3)],
        bs.at[:, pl.ds(0, 7)], sp.at[pl.ds(0, 7)], spd.at[pl.ds(0, 15)],
    )
    for i, ref in enumerate(gone):
        remote(ref, ref, send_sem.at[i], h_r.at[0], mate).wait_send()


def body(
    tokens, gate_int_codes, up_int_codes, down_int_codes, gate_column_scale, up_column_scale, down_column_scale,
    row_adapter_index, adapter_shrink_weight, adapter_expand_weight,
):
    rows, width = tokens.shape
    cols, wide = down_int_codes.shape
    shrink = jnp.transpose(adapter_shrink_weight, (0, 2, 1)).reshape(-1, cols)
    expand = adapter_expand_weight.reshape(-1, wide)
    vmem = pl.BlockSpec(memory_space=pltpu.VMEM)
    hbm = pl.BlockSpec(memory_space=pl.ANY)

    def dma(*shape):
        return pltpu.SemaphoreType.DMA(shape)

    n = BATCHES
    return pl.pallas_call(
        layer_kernel,
        out_shape=jax.ShapeDtypeStruct((rows, wide), BF16),
        in_specs=[hbm] * 10,
        out_specs=vmem,
        scratch_shapes=[
            pltpu.VMEM((cols // 128, 128), F32),
            pltpu.VMEM((cols // 128, 128), F32),
            pltpu.VMEM((wide // 128, 128), F32),
            pltpu.VMEM((8, 128), jnp.int32),
            pltpu.VMEM((2, 1, cols), F32),
            pltpu.VMEM((4, 4, 64, width), BF16),
            pltpu.VMEM((width, cols), BF16),
            pltpu.VMEM((width, cols), BF16),
            pltpu.VMEM((2, 4, 4, 64, cols), BF16),
            pltpu.VMEM((2, 2, 4, 32, cols), BF16),
            pltpu.VMEM((2, 2, 4, 64, cols), BF16),
            pltpu.VMEM((2, 2, 32, cols), BF16),
            pltpu.VMEM((2, 2, 64, cols), BF16),
            pltpu.VMEM((64, cols), F32),
            pltpu.VMEM((FACTOR, 64, 256), BF16),
            pltpu.VMEM((64, cols), BF16),
            pltpu.VMEM((n, 8, 16, PART_COLS), BF16),
            pltpu.VMEM((n, 8, 16, PART_COLS), BF16),
            pltpu.VMEM((n, 8, 16, PART_COLS), BF16),
            pltpu.VMEM((4, 4, 64, cols), BF16),
            pltpu.VMEM((cols, wide), BF16),
            pltpu.VMEM((16 * ADAPTER_RANK, cols), BF16),
            pltpu.VMEM((256 * ADAPTER_RANK, wide), BF16),
            pltpu.VMEM((n, 8, 2 * BATCH_ROWS, wide), BF16),
            pltpu.VMEM((n, 8, 2 * BATCH_ROWS, wide), BF16),
            pltpu.VMEM((8, ADAPTER_RANK, 128), F32),
            pltpu.VMEM((8, ADAPTER_RANK, 128), F32),
            pltpu.VMEM((16, ADAPTER_RANK, 128), F32),
            dma(13), dma(11), dma(n, 4), dma(n, 4), dma(n, 2, 4), dma(n, 2), dma(n), dma(n), dma(n),
            dma(n, 2), dma(n), dma(n, 4), dma(n, 4), dma(n), dma(1), dma(1),
        ],
        compiler_params=pltpu.CompilerParams(
            collective_id=0, has_side_effects=True, vmem_limit_bytes=63 * 1024 * 1024
        ),
        name="layer",
    )(
        tokens.reshape(2, 2, 32, width), gate_int_codes, up_int_codes, down_int_codes, shrink, expand,
        gate_column_scale.reshape(-1, 128), up_column_scale.reshape(-1, 128), down_column_scale.reshape(-1, 128),
        row_adapter_index.reshape(8, 128),
    )


def solution(mesh):
    return jax.shard_map(
        body,
        mesh=mesh,
        in_specs=(
            P("tensor", "dp"), P("dp", "tensor"), P("dp", "tensor"), P("tensor", "dp"), P("tensor"), P("tensor"),
            P("dp"), P(), P("dp", "tensor", None), P(None, None, "dp"),
        ),
        out_specs=P("tensor", "dp"),
        check_vma=False,
    )
```

```python
import math

import jax
import jax.numpy as jnp
import numpy as np
from jax import lax
from jax.experimental import pallas as pl
from jax.experimental.pallas import tpu as pltpu
from jax.sharding import PartitionSpec as P

FACTOR = 13
ADAPTER_RANK = 16
MESH = pl.DeviceIdType.MESH
F32, BF16 = jnp.float32, jnp.bfloat16


def sylvester_signs(order):
    i = np.arange(order)
    common = i[:, None] & i[None, :]
    parity = np.zeros_like(common)
    while common.any():
        parity ^= common & 1
        common = common >> 1
    return 1 - 2 * parity


def hartley_entries(order):
    i = np.arange(order)
    angle = 2.0 * np.pi * ((i[:, None] * i[None, :]) % order) / order
    return (np.cos(angle) + np.sin(angle)) / math.sqrt(order)


def order_of(j):
    return (2 - j + (j // 2) * (7 - 2 * j)) % 4


BATCHES = 2
BATCH_ROWS = 64 // BATCHES
HALF_ROWS = BATCH_ROWS // 2
PART_SPLIT = 8 // (BATCH_ROWS // 16)
PART_COLS = {2: 1664, 4: 896}[PART_SPLIT]


def part_place(t):
    j = t % PART_SPLIT
    first = 1664 * j if PART_SPLIT == 2 else 128 * (6 * j + (j + 2) // 3)
    return t // PART_SPLIT, first


def each(count, do):
    lax.fori_loop(0, count, lambda i, carry: (do(i), carry)[1], 0)


def layer_kernel(
    tok, wg_hbm, wu_hbm, wd_hbm, shrink_hbm, expand_hbm, sg_hbm, su_hbm, sd_hbm, ids_hbm, out,
    sgv, suv, sdv, ids, scales, xb, wg, wu, p, r1, r2, t1, t2, hid, mid, loc, am, bm, cm, rot, wd, ws, we, bs, bsr, sp, spr, spd,
    load_sem, send_sem, gr, far_r, near_r, t1_r, t2_r, a_r, c_r, g1_r, g1x_r, g2_r, g2x_r, b_r, h_r, d_r,
):
    dp, tensor = lax.axis_index("dp"), lax.axis_index("tensor")
    z, y = dp // 4, dp % 4
    x, core = tensor // 2, tensor % 2
    cols = wg.shape[1]

    def at_x(step, c):
        return (dp, ((x + step) % 4) * 2 + c)

    def at_z(step):
        return (((z + step) % 4) * 4 + y, tensor)

    def at_y(step):
        return (z * 4 + (y + step) % 4, tensor)

    def peer(i):
        return ((x + i // 2) % 4) * 2 + (core + i % 2) % 2

    def before(i):
        return ((x + 4 - i // 2) % 4) * 2 + (core + i % 2) % 2

    far_first = (4, 5, 2, 3, 6, 7, 1)

    pairs = [(tok.at[q, h], xb.at[x, 2 * core + h, pl.ds(32 * q, 32)]) for q in range(2) for h in range(2)]
    pairs += [(wg_hbm, wg), (wu_hbm, wu), (sg_hbm, sgv), (su_hbm, suv), (sd_hbm, sdv), (ids_hbm, ids)]
    pairs += [(wd_hbm, wd), (shrink_hbm, ws), (expand_hbm, we)]
    loads = [pltpu.make_async_copy(a, b, load_sem.at[i]) for i, (a, b) in enumerate(pairs)]
    for load in loads[:10]:
        load.start()

    near = [at_x(i // 2, (core + i % 2) % 2) for i in range(1, 8)]
    others = [(((z + i // 4) % 4) * 4 + (y + i % 4) % 4, tensor) for i in (10, 6, 9, 11, 14, 2, 5, 7, 8, 13, 15, 1, 3, 4, 12)]
    near += others
    barrier = pltpu.get_barrier_semaphore()
    for who in near:
        pl.semaphore_signal(barrier, inc=1, device_id=who, device_id_type=MESH)
    pl.semaphore_wait(barrier, len(near))

    def remote(src, dst, send, recv, who):
        return pltpu.make_async_remote_copy(
            src_ref=src, dst_ref=dst, send_sem=send, recv_sem=recv, device_id=who, device_id_type=MESH
        )

    mate = at_x(0, 1 - core)
    def shard(q, step, c):
        return xb.at[(x + step) % 4, pl.ds(2 * c, 2), pl.ds(32 * q, 32)]

    def await_bytes(ref, sem):
        remote(ref, ref, send_sem.at[0], sem, mate).wait_recv()

    def gather_copy(q, i, src, dst, who):
        return remote(src, dst, send_sem.at[0 if 0 < i < 4 else 1], gr.at[q, i % 4 if i < 4 else 0], who)

    def gather_start(q):
        for step in (2, 1, 3):
            gather_copy(q, step, tok.at[q], shard(q, 0, core), at_x(step, core)).start()
        gather_copy(q, 0, tok.at[q], shard(q, 0, core), mate).start()

    def gather_mate(q):
        for step in (1, 3, 2):
            ref = shard(q, 4 - step, core)
            await_bytes(ref, gr.at[q, step])
            gather_copy(q, 4, ref, ref, mate).start()

    def gather_end(q):
        await_bytes(xb.at[0], gr.at[q, 0])

    first, second = (z, y), (y, z)
    along = ((at_z, at_y), (at_y, at_z))

    def rows(q, h):
        return pl.ds(pl.multiple_of(BATCH_ROWS * q + HALF_ROWS * h, HALF_ROWS), HALF_ROWS)

    def batch_rows(q):
        return pl.ds(BATCH_ROWS * q, BATCH_ROWS)

    def half_rows(q):
        return pl.ds(HALF_ROWS * q, HALF_ROWS)

    def stage1(q, m, s, kind, k):
        step = 1 + 2 * s
        b = (second[m] + order_of(k)) % 4
        a = (first[m] + (2 if kind == 0 else step)) % 4
        h = 1 - s if kind == 1 else s
        src = p.at[m, a, b, rows(q, h)]
        dst = r1.at[m, s, b, half_rows(q)] if kind == 0 else r2.at[m, s, b, rows(q, h)]
        sem = far_r.at[q, k] if kind == 0 else near_r.at[q, m, k]
        return remote(src, dst, send_sem.at[2], sem, along[m][0](step))

    def stage2(q, m, s, kind):
        step = 1 + 2 * s
        b = (second[m] + (2 if kind == 0 else step)) % 4
        h = 1 - s if kind == 1 else s
        src = p.at[m, first[m], b, rows(q, h)]
        dst = t1.at[m, s, half_rows(q)] if kind == 0 else t2.at[m, s, rows(q, h)]
        sem = t1_r.at[q, s] if kind == 0 else t2_r.at[q]
        return remote(src, dst, send_sem.at[3], sem, along[m][1](step))

    def send_far(q, low=0, high=4):
        @pl.loop(low, high)
        def _(k):
            for m in range(2):
                for s in range(2):
                    stage1(q, m, s, 0, k).start()

    def send_near(q, s):
        @pl.loop(0, 4)
        def _(k):
            for m in range(2):
                stage1(q, m, s, 1, k).start()

    def chunk(q, j):
        for m, w in ((0, wg), (1, wu)):
            a = (first[m] + order_of(j)) % 4
            r = batch_rows(q)
            xs = (xb[a, :, r] if m == 0 else xb[:, a, r]).reshape(4 * BATCH_ROWS, xb.shape[-1])
            for n in range(cols // 256):
                block = slice(n * 256, n * 256 + 256)
                v = jnp.dot(xs, w[:, block], preferred_element_type=F32).astype(BF16)
                p[m, a, :, r, block] = v.reshape(4, BATCH_ROWS, 256)

    def first_batch(j):
        chunk(0, j)

        @pl.when(j == 0)
        def _():
            send_far(0)

        @pl.when((j == 1) | (j == 2))
        def _():
            send_near(0, j - 1)

    def second_batch(j):
        chunk(1, j)

    def spread_scales():
        for i in range(cols // 128):
            for m, ref in enumerate((sgv, suv)):
                scales[m, :, i * 128 : i * 128 + 128] = ref[i : i + 1, :]

    def add(dst, *refs):
        def group(i):
            r = pl.ds(pl.multiple_of(i * 16, 16), 16)
            v = dst[r, :].astype(F32)
            for ref in refs:
                v = v + ref[r, :].astype(F32)
            dst[r, :] = v.astype(BF16)

        each(dst.shape[0] // 16, group)

    def relay(q, k):
        await_bytes(r1.at[:, :, 0, half_rows(q)], far_r.at[q, k])
        for m in range(2):
            for s in range(2):
                b = (second[m] + order_of(k)) % 4
                add(p.at[m, (first[m] + 1 + 2 * s) % 4, b, rows(q, s)], r1.at[m, s, b, half_rows(q)])
                stage1(q, m, s, 2, k).start()

    def settle(q, m, k):
        b = (second[m] + order_of(k)) % 4
        r = batch_rows(q)
        await_bytes(r2.at[m, :, b, r], near_r.at[q, m, k])
        add(p.at[m, first[m], b, r], r2.at[m, 0, b, r], r2.at[m, 1, b, r])

    def cross_far(q):
        for m in range(2):
            settle(q, m, 0)
            for s in range(2):
                stage2(q, m, s, 0).start()

    def cross_near(q):
        for s in range(2):
            for m in range(2):
                settle(q, m, 1 + s)
                stage2(q, m, s, 1).start()

    def cross_relay(q):
        for s in range(2):
            await_bytes(t1.at[:, s, half_rows(q)], t1_r.at[q, s])
            for m in range(2):
                b = (second[m] + 1 + 2 * s) % 4
                add(p.at[m, first[m], b, rows(q, s)], t1.at[m, s, half_rows(q)])
                stage2(q, m, s, 2).start()

    def cross_end(q):
        for m in range(2):
            settle(q, m, 3)
        await_bytes(t2.at[:, :, batch_rows(q)], t2_r.at[q])

    coef = hartley_entries(FACTOR) / math.sqrt(2048)
    lanes = lax.broadcasted_iota(jnp.int32, (256, 256), 0) & lax.broadcasted_iota(jnp.int32, (256, 256), 1)
    for shift in (4, 2, 1):
        lanes = lanes ^ (lanes >> shift)
    signs = (1 - 2 * (lanes & 1)).astype(F32).astype(BF16)

    def local_part(q):
        def gated(i):
            r = pl.ds(pl.multiple_of(BATCH_ROWS * q + i * 16, 16), 16)
            g, u = (
                p[m, first[m], second[m], r, :].astype(F32) + t2[m, 0, r, :].astype(F32) + t2[m, 1, r, :].astype(F32)
                for m in range(2)
            )
            g, u = g * scales[0], u * scales[1]
            hid[r, :] = g / (1.0 + jnp.exp(-g)) * u

        each(BATCH_ROWS // 16, gated)

        def factor(i):
            r = pl.ds(pl.multiple_of(BATCH_ROWS * q + i * 16, 16), 16)
            blocks = [hid[r, a * 256 : a * 256 + 256] for a in range(FACTOR)]
            for b in range(FACTOR):
                v = blocks[0] * float(coef[b, 0])
                for a in range(1, FACTOR):
                    v = v + blocks[a] * float(coef[b, a])
                mid[b, r, :] = v.astype(BF16)

        each(BATCH_ROWS // 16, factor)
        r = batch_rows(q)
        turned = jnp.dot(
            mid[:, r, :].reshape(FACTOR * BATCH_ROWS, 256), signs, preferred_element_type=F32
        ).astype(BF16)
        for b in range(FACTOR):
            loc[r, b * 256 : b * 256 + 256] = turned[b * BATCH_ROWS : (b + 1) * BATCH_ROWS]
        for i in far_first:
            mix_copy(q, i).start()
        am[q, tensor] = my_part(q, tensor)[...]

    def my_part(q, t):
        group, start = part_place(t)
        r = pl.ds(pl.multiple_of(BATCH_ROWS * q + 16 * group, 16), 16)
        return loc.at[r, pl.ds(pl.multiple_of(start, 128), PART_COLS)]

    def mix_copy(q, i):
        to = peer(i)
        return remote(my_part(q, to), am.at[q, tensor], send_sem.at[4], a_r.at[q], (dp, to))

    def back_copy(q, i):
        to = peer(i)
        return remote(bm.at[q, to], cm.at[q, tensor], send_sem.at[5], c_r.at[q], (dp, to))

    def mix(q):
        await_bytes(am.at[q, pl.ds(0, 7)], a_r.at[q])
        for c in range(PART_COLS // 128):
            lane = slice(c * 128, c * 128 + 128)
            v = [am[q, t, :, lane].astype(F32) for t in range(8)]
            for bit in (1, 2, 4):
                v = [v[t] + v[t ^ bit] if t & bit == 0 else v[t ^ bit] - v[t] for t in range(8)]
            for t in range(8):
                bm[q, t, :, lane] = v[t].astype(BF16)
        for i in far_first:
            back_copy(q, i).start()
        cm[q, tensor] = bm[q, tensor]

    def off(c):
        return c + (c // 2) * (5 - 2 * c)

    def held(q, f, c1, c2):
        c = (c1 % 4, c2 % 4) if f == 0 else (c2 % 4, c1 % 4)
        return rot.at[c[0], c[1], rows(q, f)]

    def half_cols(s):
        return pl.ds(s * (cols // 2), cols // 2)

    def spread1(q, f, s, kind):
        step = 1 + 2 * s
        ref = held(q, f, first[f] + (0 if kind == 0 else 4 - step), second[f])
        if kind == 1:
            ref = ref.at[:, half_cols(s)]
        sem = g1_r.at[q, s] if kind == 0 else g1x_r.at[q]
        return remote(ref, ref, send_sem.at[6], sem, along[f][0](step))

    def spread2(q, f, s, kind, c):
        step = 1 + 2 * s
        ref = held(q, f, first[f] + off(c), second[f] + (0 if kind == 0 else 4 - step))
        if kind == 1:
            ref = ref.at[:, half_cols(s)]
        sem = g2_r.at[q, c] if kind == 0 else g2x_r.at[q, c]
        return remote(ref, ref, send_sem.at[7], sem, along[f][1](step))

    def spread_start(q):
        await_bytes(cm.at[q, pl.ds(0, 7)], c_r.at[q])
        for t in range(8):
            group, start = part_place(t)
            r = pl.ds(BATCH_ROWS * q + 16 * group, 16)
            rot[z, y, r, start : start + PART_COLS] = cm[q, t]
        for f in range(2):
            for s in range(2):
                spread1(q, f, s, 0).start()
        for f in range(2):
            for s in range(2):
                spread2(q, f, s, 0, 0).start()

    def spread_mid(q):
        for s in range(2):
            await_bytes(rot.at[0, 0, batch_rows(q)], g1_r.at[q, s])
            for f in range(2):
                spread1(q, f, s, 1).start()
        for s in range(2):
            for f in range(2):
                for s2 in range(2):
                    spread2(q, f, s2, 0, 2 - s).start()

    def spread_far(q):
        await_bytes(rot.at[0, 0, batch_rows(q)], g1x_r.at[q])
        for f in range(2):
            for s2 in range(2):
                spread2(q, f, s2, 0, 3).start()

    def spread_relay(q, c):
        await_bytes(rot.at[0, 0], g2_r.at[q, c])
        for f in range(2):
            for s in range(2):
                spread2(q, f, s, 1, c).start()

    def spread_end(q):
        for c in range(4):
            await_bytes(rot.at[0, 0, batch_rows(q)], g2x_r.at[q, c])

    def sum_piece(q, c1, c2):
        to = 2 * c1 + c2 // 2
        r = pl.ds(pl.multiple_of(BATCH_ROWS * (c2 % 2), BATCH_ROWS), BATCH_ROWS)
        return remote(bs.at[q, to, r], bsr.at[q, tensor, r], send_sem.at[8], b_r.at[q], (dp, to)), to, r

    def ids_of(t):
        row = ids[0:1, :]
        for i in range(1, 8):
            row = jnp.where(t == i, ids[i : i + 1, :], row)
        return row

    lane = lax.broadcasted_iota(jnp.int32, (ADAPTER_RANK, 128), 1)

    def shrink(q, c):
        lhs = rot[c, :, batch_rows(q), :].reshape(4 * BATCH_ROWS, cols)
        parts = lax.dot_general(ws[...], lhs, (((1,), (1,)), ((), ())), preferred_element_type=F32)
        even, odd = 2 * c, 2 * c + 1
        if q == 0:
            id_row = jnp.where(lane[:1] < 64, ids_of(even), pltpu.roll(ids_of(odd), 64, 1))
        else:
            id_row = jnp.where(lane[:1] < 64, pltpu.roll(ids_of(even), 64, 1), ids_of(odd))
        v = jnp.zeros((ADAPTER_RANK, 128), F32)
        for a in range(16):
            v = v + jnp.where(id_row == dp * 16 + a, parts[a * 16 : a * 16 + 16], 0.0)
        turned = pltpu.roll(v, 64, 1)
        if q == 0:
            sp[even] = v
            sp[odd] = turned
        else:
            sp[even] = jnp.where(lane < 64, sp[even], turned)
            sp[odd] = jnp.where(lane < 64, sp[odd], v)

    def shrink_all(q):
        each(4, lambda c: shrink(q, c))

    def shrink_send():
        for i in far_first:
            shrink_copy(i).start()

    def down(q, places):
        places = [((z + i) % 4, (y + j) % 4) for i, j in places]
        lhs = jnp.concatenate([rot[c1, c2, batch_rows(q)] for c1, c2 in places], axis=0)
        base = jnp.dot(lhs, wd[...], preferred_element_type=F32).astype(BF16)
        for n, (c1, c2) in enumerate(places):
            copy, to, r = sum_piece(q, c1, c2)
            bs[q, to, r] = base[n * BATCH_ROWS : (n + 1) * BATCH_ROWS]

            @pl.when(to != tensor)
            def _():
                copy.start()

    def down_early(q):
        down(q, [(i, j) for j in (0, 1, 3) for i in (0, 1, 3)])

    def down_late(q):
        down(q, [(2, j) for j in range(4)] + [(i, 2) for i in (0, 1, 3)])

    def shrink_copy(i):
        to = peer(i)
        return remote(sp.at[to], spr.at[tensor], send_sem.at[9], h_r.at[0], (dp, to))

    def shrink_across(who):
        return remote(spd.at[dp], spd.at[dp], send_sem.at[10], d_r.at[0], who)

    def total(refs):
        v = refs[0]
        for ref in refs[1:]:
            v = v + ref
        return v

    def finish():
        await_bytes(spr.at[pl.ds(0, 7)], h_r.at[0])
        spr[tensor] = sp[tensor]
        spd[dp] = total([spr[t] for t in range(8)])
        for who in others:
            shrink_across(who).start()
        bases = []
        for q in range(BATCHES):
            await_bytes(bsr.at[q, pl.ds(0, 7)], b_r.at[q])
            bsr[q, tensor] = bs[q, tensor]
            bases.append(total([bsr[q, t].astype(F32) for t in range(8)]))
        await_bytes(spd.at[pl.ds(0, 15)], d_r.at[0])
        shrunk = total([spd[c] for c in range(16)])
        wide = jnp.concatenate([shrunk] * 8, axis=0).T
        own_ids = jnp.broadcast_to(ids_of(tensor), (128, 128)).astype(F32).T
        lane_adapter = (lax.broadcasted_iota(jnp.int32, (128, 128), 1) // ADAPTER_RANK).astype(F32)
        spot = own_ids - lane_adapter
        chosen = jnp.concatenate(
            [jnp.where(spot == float(8 * j), wide, 0.0).astype(BF16) for j in range(32)], axis=1
        )
        extra = jnp.dot(chosen, we[...], preferred_element_type=F32)
        for q in range(BATCHES):
            r = slice(2 * BATCH_ROWS * q, 2 * BATCH_ROWS * (q + 1))
            base = bases[q]
            for i in range(out.shape[1] // 128):
                block = slice(i * 128, i * 128 + 128)
                out[r, block] = (base[:, block] * sdv[i : i + 1, :] + extra[r, block]).astype(BF16)

    gather_start(0)
    gather_mate(0)
    for load in loads[:6]:
        load.wait()
    gather_end(0)
    gather_start(1)
    each(4, first_batch)
    gather_mate(1)
    gather_end(1)
    for load in loads[10:]:
        load.start()
    each(4, second_batch)
    for load in loads[6:10]:
        load.wait()
    spread_scales()
    send_far(1, 0, 2)
    relay(0, 0)
    relay(0, 1)
    relay(0, 2)
    relay(0, 3)
    cross_far(0)
    cross_near(0)
    relay(1, 0)
    relay(1, 1)
    send_far(1, 2, 4)
    cross_relay(0)
    send_near(1, 0)
    send_near(1, 1)
    relay(1, 2)
    cross_end(0)
    relay(1, 3)
    cross_far(1)
    local_part(0)
    cross_near(1)
    mix(0)
    cross_relay(1)
    spread_start(0)
    cross_end(1)
    local_part(1)
    spread_mid(0)
    mix(1)
    spread_far(0)
    spread_relay(0, 1)
    spread_relay(0, 0)
    spread_relay(0, 2)
    spread_start(1)
    for load in loads[10:]:
        load.wait()
    spread_relay(0, 3)
    spread_mid(1)
    down_early(0)
    spread_end(0)
    spread_far(1)
    shrink_all(0)
    spread_relay(1, 1)
    down_late(0)
    spread_relay(1, 2)
    spread_relay(1, 0)
    spread_relay(1, 3)
    down_early(1)
    spread_end(1)
    shrink_all(1)
    shrink_send()
    down_late(1)
    finish()

    gone = (
        xb.at[pl.ds(0, 2), pl.ds(0, 3)], xb.at[pl.ds(0, 2)], p.at[:, pl.ds(0, 3)], p.at[0, pl.ds(0, 2), pl.ds(0, 3)],
        am.at[:, pl.ds(0, 7)], cm.at[:, pl.ds(0, 7)], rot.at[0, pl.ds(0, 3)], rot.at[pl.ds(0, 3)],
        bs.at[:, pl.ds(0, 7)], sp.at[pl.ds(0, 7)], spd.at[pl.ds(0, 15)],
    )
    for i, ref in enumerate(gone):
        remote(ref, ref, send_sem.at[i], h_r.at[0], mate).wait_send()


def body(
    tokens, gate_int_codes, up_int_codes, down_int_codes, gate_column_scale, up_column_scale, down_column_scale,
    row_adapter_index, adapter_shrink_weight, adapter_expand_weight,
):
    rows, width = tokens.shape
    cols, wide = down_int_codes.shape
    shrink = jnp.transpose(adapter_shrink_weight, (0, 2, 1)).reshape(-1, cols)
    expand = adapter_expand_weight.reshape(-1, wide)
    vmem = pl.BlockSpec(memory_space=pltpu.VMEM)
    hbm = pl.BlockSpec(memory_space=pl.ANY)

    def dma(*shape):
        return pltpu.SemaphoreType.DMA(shape)

    n = BATCHES
    return pl.pallas_call(
        layer_kernel,
        out_shape=jax.ShapeDtypeStruct((rows, wide), BF16),
        in_specs=[hbm] * 10,
        out_specs=vmem,
        scratch_shapes=[
            pltpu.VMEM((cols // 128, 128), F32),
            pltpu.VMEM((cols // 128, 128), F32),
            pltpu.VMEM((wide // 128, 128), F32),
            pltpu.VMEM((8, 128), jnp.int32),
            pltpu.VMEM((2, 1, cols), F32),
            pltpu.VMEM((4, 4, 64, width), BF16),
            pltpu.VMEM((width, cols), BF16),
            pltpu.VMEM((width, cols), BF16),
            pltpu.VMEM((2, 4, 4, 64, cols), BF16),
            pltpu.VMEM((2, 2, 4, 32, cols), BF16),
            pltpu.VMEM((2, 2, 4, 64, cols), BF16),
            pltpu.VMEM((2, 2, 32, cols), BF16),
            pltpu.VMEM((2, 2, 64, cols), BF16),
            pltpu.VMEM((64, cols), F32),
            pltpu.VMEM((FACTOR, 64, 256), BF16),
            pltpu.VMEM((64, cols), BF16),
            pltpu.VMEM((n, 8, 16, PART_COLS), BF16),
            pltpu.VMEM((n, 8, 16, PART_COLS), BF16),
            pltpu.VMEM((n, 8, 16, PART_COLS), BF16),
            pltpu.VMEM((4, 4, 64, cols), BF16),
            pltpu.VMEM((cols, wide), BF16),
            pltpu.VMEM((16 * ADAPTER_RANK, cols), BF16),
            pltpu.VMEM((256 * ADAPTER_RANK, wide), BF16),
            pltpu.VMEM((n, 8, 2 * BATCH_ROWS, wide), BF16),
            pltpu.VMEM((n, 8, 2 * BATCH_ROWS, wide), BF16),
            pltpu.VMEM((8, ADAPTER_RANK, 128), F32),
            pltpu.VMEM((8, ADAPTER_RANK, 128), F32),
            pltpu.VMEM((16, ADAPTER_RANK, 128), F32),
            dma(13), dma(11), dma(n, 4), dma(n, 4), dma(n, 2, 4), dma(n, 2), dma(n), dma(n), dma(n),
            dma(n, 2), dma(n), dma(n, 4), dma(n, 4), dma(n), dma(1), dma(1),
        ],
        compiler_params=pltpu.CompilerParams(
            collective_id=0, has_side_effects=True, vmem_limit_bytes=63 * 1024 * 1024
        ),
        name="layer",
    )(
        tokens.reshape(2, 2, 32, width), gate_int_codes, up_int_codes, down_int_codes, shrink, expand,
        gate_column_scale.reshape(-1, 128), up_column_scale.reshape(-1, 128), down_column_scale.reshape(-1, 128),
        row_adapter_index.reshape(8, 128),
    )


def solution(mesh):
    return jax.shard_map(
        body,
        mesh=mesh,
        in_specs=(
            P("tensor", "dp"), P("dp", "tensor"), P("dp", "tensor"), P("tensor", "dp"), P("tensor"), P("tensor"),
            P("dp"), P(), P("dp", "tensor", None), P(None, None, "dp"),
        ),
        out_specs=P("tensor", "dp"),
        check_vma=False,
    )
```

```python
import math

import jax
import jax.numpy as jnp
import numpy as np
from jax import lax
from jax.experimental import pallas as pl
from jax.experimental.pallas import tpu as pltpu
from jax.sharding import PartitionSpec as P

FACTOR = 13
ADAPTER_RANK = 16
MESH = pl.DeviceIdType.MESH
F32, BF16 = jnp.float32, jnp.bfloat16


def sylvester_signs(order):
    i = np.arange(order)
    common = i[:, None] & i[None, :]
    parity = np.zeros_like(common)
    while common.any():
        parity ^= common & 1
        common = common >> 1
    return 1 - 2 * parity


def hartley_entries(order):
    i = np.arange(order)
    angle = 2.0 * np.pi * ((i[:, None] * i[None, :]) % order) / order
    return (np.cos(angle) + np.sin(angle)) / math.sqrt(order)


def order_of(j):
    return (2 - j + (j // 2) * (7 - 2 * j)) % 4


BATCHES = 2
BATCH_ROWS = 64 // BATCHES
HALF_ROWS = BATCH_ROWS // 2
PART_SPLIT = 8 // (BATCH_ROWS // 16)
PART_COLS = {2: 1664, 4: 896}[PART_SPLIT]


def part_place(t):
    j = t % PART_SPLIT
    first = 1664 * j if PART_SPLIT == 2 else 128 * (6 * j + (j + 2) // 3)
    return t // PART_SPLIT, first


def each(count, do):
    lax.fori_loop(0, count, lambda i, carry: (do(i), carry)[1], 0)


def layer_kernel(
    tok, wg_hbm, wu_hbm, wd_hbm, shrink_hbm, expand_hbm, sg_hbm, su_hbm, sd_hbm, ids_hbm, out,
    sgv, suv, sdv, ids, scales, signs, xb, wg, wu, p, r1, r2, t1, t2, hid, mid, loc, am, bm, cm, rot, wd, ws, we, bs, bsr, sp, spr, spd,
    load_sem, send_sem, gr, far_r, near_r, t1_r, t2_r, a_r, c_r, g1_r, g1x_r, g2_r, g2x_r, b_r, h_r, d_r,
):
    dp, tensor = lax.axis_index("dp"), lax.axis_index("tensor")
    z, y = dp // 4, dp % 4
    x, core = tensor // 2, tensor % 2
    cols = wg.shape[1]

    def at_x(step, c):
        return (dp, ((x + step) % 4) * 2 + c)

    def at_z(step):
        return (((z + step) % 4) * 4 + y, tensor)

    def at_y(step):
        return (z * 4 + (y + step) % 4, tensor)

    def peer(i):
        return ((x + i // 2) % 4) * 2 + (core + i % 2) % 2

    def before(i):
        return ((x + 4 - i // 2) % 4) * 2 + (core + i % 2) % 2

    far_first = (4, 5, 2, 3, 6, 7, 1)

    pairs = [(tok.at[q, h], xb.at[x, 2 * core + h, pl.ds(32 * q, 32)]) for q in range(2) for h in range(2)]
    pairs += [(wg_hbm, wg), (wu_hbm, wu), (sg_hbm, sgv), (su_hbm, suv), (sd_hbm, sdv), (ids_hbm, ids)]
    pairs += [(wd_hbm, wd), (shrink_hbm, ws), (expand_hbm, we)]
    loads = [pltpu.make_async_copy(a, b, load_sem.at[i]) for i, (a, b) in enumerate(pairs)]
    near = [at_x(i // 2, (core + i % 2) % 2) for i in range(1, 8)]
    others = [(((z + i // 4) % 4) * 4 + (y + i % 4) % 4, tensor) for i in (10, 6, 9, 11, 14, 2, 5, 7, 8, 13, 15, 1, 3, 4, 12)]
    near += others
    barrier = pltpu.get_barrier_semaphore()
    for who in near:
        pl.semaphore_signal(barrier, inc=1, device_id=who, device_id_type=MESH)
    for load in loads[:10]:
        load.start()
    pl.semaphore_wait(barrier, len(near))

    def remote(src, dst, send, recv, who):
        return pltpu.make_async_remote_copy(
            src_ref=src, dst_ref=dst, send_sem=send, recv_sem=recv, device_id=who, device_id_type=MESH
        )

    mate = at_x(0, 1 - core)
    def shard(q, step, c):
        return xb.at[(x + step) % 4, pl.ds(2 * c, 2), pl.ds(32 * q, 32)]

    def await_bytes(ref, sem):
        remote(ref, ref, send_sem.at[0], sem, mate).wait_recv()

    def gather_copy(q, i, src, dst, who):
        return remote(src, dst, send_sem.at[0 if 0 < i < 4 else 1], gr.at[q, i % 4 if i < 4 else 0], who)

    def gather_start(q):
        for step in (2, 1, 3):
            gather_copy(q, step, tok.at[q], shard(q, 0, core), at_x(step, core)).start()
        gather_copy(q, 0, tok.at[q], shard(q, 0, core), mate).start()

    def gather_mate(q):
        for step in (1, 3, 2):
            ref = shard(q, 4 - step, core)
            await_bytes(ref, gr.at[q, step])
            gather_copy(q, 4, ref, ref, mate).start()

    def gather_end(q):
        await_bytes(xb.at[0], gr.at[q, 0])

    first, second = (z, y), (y, z)
    along = ((at_z, at_y), (at_y, at_z))

    def rows(q, h):
        return pl.ds(pl.multiple_of(BATCH_ROWS * q + HALF_ROWS * h, HALF_ROWS), HALF_ROWS)

    def batch_rows(q):
        return pl.ds(BATCH_ROWS * q, BATCH_ROWS)

    def half_rows(q):
        return pl.ds(HALF_ROWS * q, HALF_ROWS)

    def stage1(q, m, s, kind, k):
        step = 1 + 2 * s
        b = (second[m] + order_of(k)) % 4
        a = (first[m] + (2 if kind == 0 else step)) % 4
        h = 1 - s if kind == 1 else s
        src = p.at[m, a, b, rows(q, h)]
        dst = r1.at[m, s, b, half_rows(q)] if kind == 0 else r2.at[m, s, b, rows(q, h)]
        sem = far_r.at[q, k] if kind == 0 else near_r.at[q, m, k]
        return remote(src, dst, send_sem.at[2], sem, along[m][0](step))

    def stage2(q, m, s, kind):
        step = 1 + 2 * s
        b = (second[m] + (2 if kind == 0 else step)) % 4
        h = 1 - s if kind == 1 else s
        src = p.at[m, first[m], b, rows(q, h)]
        dst = t1.at[m, s, half_rows(q)] if kind == 0 else t2.at[m, s, rows(q, h)]
        sem = t1_r.at[q, s] if kind == 0 else t2_r.at[q]
        return remote(src, dst, send_sem.at[3], sem, along[m][1](step))

    def send_far(q, low=0, high=4):
        @pl.loop(low, high)
        def _(k):
            for m in range(2):
                for s in range(2):
                    stage1(q, m, s, 0, k).start()

    def send_near(q, s):
        @pl.loop(0, 4)
        def _(k):
            for m in range(2):
                stage1(q, m, s, 1, k).start()

    def chunk(q, j):
        for m, w in ((0, wg), (1, wu)):
            a = (first[m] + order_of(j)) % 4
            r = batch_rows(q)
            xs = (xb[a, :, r] if m == 0 else xb[:, a, r]).reshape(4 * BATCH_ROWS, xb.shape[-1])
            for n in range(cols // 256):
                block = slice(n * 256, n * 256 + 256)
                v = jnp.dot(xs, w[:, block], preferred_element_type=F32).astype(BF16)
                p[m, a, :, r, block] = v.reshape(4, BATCH_ROWS, 256)

    def first_batch(j):
        chunk(0, j)

        @pl.when(j == 0)
        def _():
            send_far(0)

        @pl.when((j == 1) | (j == 2))
        def _():
            send_near(0, j - 1)

    def second_batch(j):
        chunk(1, j)

    def spread_scales():
        lanes = lax.broadcasted_iota(jnp.int32, (256, 256), 0) & lax.broadcasted_iota(jnp.int32, (256, 256), 1)
        for shift in (4, 2, 1):
            lanes = lanes ^ (lanes >> shift)
        signs[...] = (1 - 2 * (lanes & 1)).astype(F32).astype(BF16)
        for i in range(cols // 128):
            for m, ref in enumerate((sgv, suv)):
                scales[m, :, i * 128 : i * 128 + 128] = ref[i : i + 1, :]

    def add(dst, *refs):
        def group(i):
            r = pl.ds(pl.multiple_of(i * 16, 16), 16)
            v = dst[r, :].astype(F32)
            for ref in refs:
                v = v + ref[r, :].astype(F32)
            dst[r, :] = v.astype(BF16)

        each(dst.shape[0] // 16, group)

    def relay(q, k):
        await_bytes(r1.at[:, :, 0, half_rows(q)], far_r.at[q, k])
        for m in range(2):
            for s in range(2):
                b = (second[m] + order_of(k)) % 4
                add(p.at[m, (first[m] + 1 + 2 * s) % 4, b, rows(q, s)], r1.at[m, s, b, half_rows(q)])
                stage1(q, m, s, 2, k).start()

    def settle(q, m, k):
        b = (second[m] + order_of(k)) % 4
        r = batch_rows(q)
        await_bytes(r2.at[m, :, b, r], near_r.at[q, m, k])
        add(p.at[m, first[m], b, r], r2.at[m, 0, b, r], r2.at[m, 1, b, r])

    def cross_far(q):
        for m in range(2):
            settle(q, m, 0)
            for s in range(2):
                stage2(q, m, s, 0).start()

    def cross_near(q):
        for s in range(2):
            for m in range(2):
                settle(q, m, 1 + s)
                stage2(q, m, s, 1).start()

    def cross_relay(q):
        for s in range(2):
            await_bytes(t1.at[:, s, half_rows(q)], t1_r.at[q, s])
            for m in range(2):
                b = (second[m] + 1 + 2 * s) % 4
                add(p.at[m, first[m], b, rows(q, s)], t1.at[m, s, half_rows(q)])
                stage2(q, m, s, 2).start()

    def cross_end(q):
        for m in range(2):
            settle(q, m, 3)
        await_bytes(t2.at[:, :, batch_rows(q)], t2_r.at[q])

    coef = hartley_entries(FACTOR) / math.sqrt(2048)
    def local_part(q):
        def gated(i):
            r = pl.ds(pl.multiple_of(BATCH_ROWS * q + i * 16, 16), 16)
            g, u = (
                p[m, first[m], second[m], r, :].astype(F32) + t2[m, 0, r, :].astype(F32) + t2[m, 1, r, :].astype(F32)
                for m in range(2)
            )
            g, u = g * scales[0], u * scales[1]
            hid[r, :] = g / (1.0 + jnp.exp(-g)) * u

        each(BATCH_ROWS // 16, gated)

        def factor(i):
            r = pl.ds(pl.multiple_of(BATCH_ROWS * q + i * 16, 16), 16)
            blocks = [hid[r, a * 256 : a * 256 + 256] for a in range(FACTOR)]
            for b in range(FACTOR):
                v = blocks[0] * float(coef[b, 0])
                for a in range(1, FACTOR):
                    v = v + blocks[a] * float(coef[b, a])
                mid[b, r, :] = v.astype(BF16)

        each(BATCH_ROWS // 16, factor)
        r = batch_rows(q)
        turned = jnp.dot(
            mid[:, r, :].reshape(FACTOR * BATCH_ROWS, 256), signs[...], preferred_element_type=F32
        ).astype(BF16)
        for b in range(FACTOR):
            loc[r, b * 256 : b * 256 + 256] = turned[b * BATCH_ROWS : (b + 1) * BATCH_ROWS]
        for i in far_first:
            mix_copy(q, i).start()
        am[q, tensor] = my_part(q, tensor)[...]

    def my_part(q, t):
        group, start = part_place(t)
        r = pl.ds(pl.multiple_of(BATCH_ROWS * q + 16 * group, 16), 16)
        return loc.at[r, pl.ds(pl.multiple_of(start, 128), PART_COLS)]

    def mix_copy(q, i):
        to = peer(i)
        return remote(my_part(q, to), am.at[q, tensor], send_sem.at[4], a_r.at[q], (dp, to))

    def back_copy(q, i):
        to = peer(i)
        return remote(bm.at[q, to], cm.at[q, tensor], send_sem.at[5], c_r.at[q], (dp, to))

    def mix(q):
        await_bytes(am.at[q, pl.ds(0, 7)], a_r.at[q])
        for c in range(PART_COLS // 128):
            lane = slice(c * 128, c * 128 + 128)
            v = [am[q, t, :, lane].astype(F32) for t in range(8)]
            for bit in (1, 2, 4):
                v = [v[t] + v[t ^ bit] if t & bit == 0 else v[t ^ bit] - v[t] for t in range(8)]
            for t in range(8):
                bm[q, t, :, lane] = v[t].astype(BF16)
        for i in far_first:
            back_copy(q, i).start()
        cm[q, tensor] = bm[q, tensor]

    def off(c):
        return c + (c // 2) * (5 - 2 * c)

    def held(q, f, c1, c2):
        c = (c1 % 4, c2 % 4) if f == 0 else (c2 % 4, c1 % 4)
        return rot.at[c[0], c[1], rows(q, f)]

    def half_cols(s):
        return pl.ds(s * (cols // 2), cols // 2)

    def spread1(q, f, s, kind):
        step = 1 + 2 * s
        ref = held(q, f, first[f] + (0 if kind == 0 else 4 - step), second[f])
        if kind == 1:
            ref = ref.at[:, half_cols(s)]
        sem = g1_r.at[q, s] if kind == 0 else g1x_r.at[q]
        return remote(ref, ref, send_sem.at[6], sem, along[f][0](step))

    def spread2(q, f, s, kind, c):
        step = 1 + 2 * s
        ref = held(q, f, first[f] + off(c), second[f] + (0 if kind == 0 else 4 - step))
        if kind == 1:
            ref = ref.at[:, half_cols(s)]
        sem = g2_r.at[q, c] if kind == 0 else g2x_r.at[q, c]
        return remote(ref, ref, send_sem.at[7], sem, along[f][1](step))

    def spread_start(q):
        await_bytes(cm.at[q, pl.ds(0, 7)], c_r.at[q])
        for t in range(8):
            group, start = part_place(t)
            r = pl.ds(BATCH_ROWS * q + 16 * group, 16)
            rot[z, y, r, start : start + PART_COLS] = cm[q, t]
        for f in range(2):
            for s in range(2):
                spread1(q, f, s, 0).start()
        for f in range(2):
            for s in range(2):
                spread2(q, f, s, 0, 0).start()

    def spread_mid(q):
        for s in range(2):
            await_bytes(rot.at[0, 0, batch_rows(q)], g1_r.at[q, s])
            for f in range(2):
                spread1(q, f, s, 1).start()
        for s in range(2):
            for f in range(2):
                for s2 in range(2):
                    spread2(q, f, s2, 0, 2 - s).start()

    def spread_far(q):
        await_bytes(rot.at[0, 0, batch_rows(q)], g1x_r.at[q])
        for f in range(2):
            for s2 in range(2):
                spread2(q, f, s2, 0, 3).start()

    def spread_relay(q, c):
        await_bytes(rot.at[0, 0], g2_r.at[q, c])
        for f in range(2):
            for s in range(2):
                spread2(q, f, s, 1, c).start()

    def spread_end(q):
        for c in range(4):
            await_bytes(rot.at[0, 0, batch_rows(q)], g2x_r.at[q, c])

    def sum_piece(q, c1, c2):
        to = 2 * c1 + c2 // 2
        r = pl.ds(pl.multiple_of(BATCH_ROWS * (c2 % 2), BATCH_ROWS), BATCH_ROWS)
        return remote(bs.at[q, to, r], bsr.at[q, tensor, r], send_sem.at[8], b_r.at[q], (dp, to)), to, r

    def ids_of(t):
        row = ids[0:1, :]
        for i in range(1, 8):
            row = jnp.where(t == i, ids[i : i + 1, :], row)
        return row

    lane = lax.broadcasted_iota(jnp.int32, (ADAPTER_RANK, 128), 1)

    def shrink(q, g):
        lhs = rot[pl.ds(2 * g, 2), :, batch_rows(q), :].reshape(8 * BATCH_ROWS, cols)
        both = lax.dot_general(ws[...], lhs, (((1,), (1,)), ((), ())), preferred_element_type=F32)
        for i in range(2):
            parts = both[:, i * 128 : i * 128 + 128]
            even, odd = 4 * g + 2 * i, 4 * g + 2 * i + 1
            if q == 0:
                id_row = jnp.where(lane[:1] < 64, ids_of(even), pltpu.roll(ids_of(odd), 64, 1))
            else:
                id_row = jnp.where(lane[:1] < 64, pltpu.roll(ids_of(even), 64, 1), ids_of(odd))
            v = jnp.zeros((ADAPTER_RANK, 128), F32)
            for a in range(16):
                v = v + jnp.where(id_row == dp * 16 + a, parts[a * 16 : a * 16 + 16], 0.0)
            turned = pltpu.roll(v, 64, 1)
            if q == 0:
                sp[even] = v
                sp[odd] = turned
            else:
                sp[even] = jnp.where(lane < 64, sp[even], turned)
                sp[odd] = jnp.where(lane < 64, sp[odd], v)

    def shrink_all(q):
        for g in range(2):
            shrink(q, g)

    def shrink_send():
        for i in far_first:
            shrink_copy(i).start()

    def down(q, places):
        places = [((z + i) % 4, (y + j) % 4) for i, j in places]
        lhs = jnp.concatenate([rot[c1, c2, batch_rows(q)] for c1, c2 in places], axis=0)
        base = jnp.dot(lhs, wd[...], preferred_element_type=F32).astype(BF16)
        for n, (c1, c2) in enumerate(places):
            copy, to, r = sum_piece(q, c1, c2)
            bs[q, to, r] = base[n * BATCH_ROWS : (n + 1) * BATCH_ROWS]

            @pl.when(to != tensor)
            def _():
                copy.start()

    def down_early(q):
        down(q, [(i, j) for j in (0, 1, 3) for i in (0, 1, 3)])

    def down_late(q):
        down(q, [(2, j) for j in range(4)] + [(i, 2) for i in (0, 1, 3)])

    def shrink_copy(i):
        to = peer(i)
        return remote(sp.at[to], spr.at[tensor], send_sem.at[9], h_r.at[0], (dp, to))

    def shrink_across(who):
        return remote(spd.at[dp], spd.at[dp], send_sem.at[10], d_r.at[0], who)

    def total(refs):
        v = refs[0]
        for ref in refs[1:]:
            v = v + ref
        return v

    def finish():
        await_bytes(spr.at[pl.ds(0, 7)], h_r.at[0])
        spr[tensor] = sp[tensor]
        spd[dp] = total([spr[t] for t in range(8)])
        for who in others:
            shrink_across(who).start()
        bases = []
        for q in range(BATCHES):
            await_bytes(bsr.at[q, pl.ds(0, 7)], b_r.at[q])
            bsr[q, tensor] = bs[q, tensor]
            bases.append(total([bsr[q, t].astype(F32) for t in range(8)]))
        await_bytes(spd.at[pl.ds(0, 15)], d_r.at[0])
        shrunk = total([spd[c] for c in range(16)])
        wide = jnp.concatenate([shrunk] * 8, axis=0).T
        own_ids = jnp.broadcast_to(ids_of(tensor), (128, 128)).astype(F32).T
        lane_adapter = (lax.broadcasted_iota(jnp.int32, (128, 128), 1) // ADAPTER_RANK).astype(F32)
        spot = own_ids - lane_adapter
        chosen = jnp.concatenate(
            [jnp.where(spot == float(8 * j), wide, 0.0).astype(BF16) for j in range(32)], axis=1
        )
        extra = jnp.dot(chosen, we[...], preferred_element_type=F32)
        for q in range(BATCHES):
            r = slice(2 * BATCH_ROWS * q, 2 * BATCH_ROWS * (q + 1))
            base = bases[q]
            for i in range(out.shape[1] // 128):
                block = slice(i * 128, i * 128 + 128)
                out[r, block] = (base[:, block] * sdv[i : i + 1, :] + extra[r, block]).astype(BF16)

    gather_start(0)
    gather_mate(0)
    for load in loads[:6]:
        load.wait()
    gather_end(0)
    gather_start(1)
    each(4, first_batch)
    gather_mate(1)
    gather_end(1)
    for load in loads[10:]:
        load.start()
    each(4, second_batch)
    for load in loads[6:10]:
        load.wait()
    spread_scales()
    send_far(1, 0, 2)
    relay(0, 0)
    relay(0, 1)
    relay(0, 2)
    relay(0, 3)
    cross_far(0)
    cross_near(0)
    relay(1, 0)
    relay(1, 1)
    send_far(1, 2, 4)
    cross_relay(0)
    send_near(1, 0)
    send_near(1, 1)
    relay(1, 2)
    cross_end(0)
    relay(1, 3)
    cross_far(1)
    local_part(0)
    cross_near(1)
    mix(0)
    cross_relay(1)
    spread_start(0)
    cross_end(1)
    local_part(1)
    spread_mid(0)
    mix(1)
    spread_far(0)
    spread_relay(0, 1)
    spread_relay(0, 0)
    spread_relay(0, 2)
    spread_start(1)
    for load in loads[10:]:
        load.wait()
    spread_relay(0, 3)
    spread_mid(1)
    down_early(0)
    spread_end(0)
    spread_far(1)
    shrink_all(0)
    spread_relay(1, 1)
    down_late(0)
    spread_relay(1, 2)
    spread_relay(1, 0)
    spread_relay(1, 3)
    down_early(1)
    spread_end(1)
    shrink_all(1)
    shrink_send()
    down_late(1)
    finish()

    gone = (
        xb.at[pl.ds(0, 2), pl.ds(0, 3)], xb.at[pl.ds(0, 2)], p.at[:, pl.ds(0, 3)], p.at[0, pl.ds(0, 2), pl.ds(0, 3)],
        am.at[:, pl.ds(0, 7)], cm.at[:, pl.ds(0, 7)], rot.at[0, pl.ds(0, 3)], rot.at[pl.ds(0, 3)],
        bs.at[:, pl.ds(0, 7)], sp.at[pl.ds(0, 7)], spd.at[pl.ds(0, 15)],
    )
    for i, ref in enumerate(gone):
        remote(ref, ref, send_sem.at[i], h_r.at[0], mate).wait_send()


def body(
    tokens, gate_int_codes, up_int_codes, down_int_codes, gate_column_scale, up_column_scale, down_column_scale,
    row_adapter_index, adapter_shrink_weight, adapter_expand_weight,
):
    rows, width = tokens.shape
    cols, wide = down_int_codes.shape
    shrink = jnp.transpose(adapter_shrink_weight, (0, 2, 1)).reshape(-1, cols)
    expand = adapter_expand_weight.reshape(-1, wide)
    vmem = pl.BlockSpec(memory_space=pltpu.VMEM)
    hbm = pl.BlockSpec(memory_space=pl.ANY)

    def dma(*shape):
        return pltpu.SemaphoreType.DMA(shape)

    n = BATCHES
    return pl.pallas_call(
        layer_kernel,
        out_shape=pltpu.VMEM((rows, wide), BF16),
        in_specs=[hbm] * 10,
        out_specs=vmem,
        scratch_shapes=[
            pltpu.VMEM((cols // 128, 128), F32),
            pltpu.VMEM((cols // 128, 128), F32),
            pltpu.VMEM((wide // 128, 128), F32),
            pltpu.VMEM((8, 128), jnp.int32),
            pltpu.VMEM((2, 1, cols), F32),
            pltpu.VMEM((256, 256), BF16),
            pltpu.VMEM((4, 4, 64, width), BF16),
            pltpu.VMEM((width, cols), BF16),
            pltpu.VMEM((width, cols), BF16),
            pltpu.VMEM((2, 4, 4, 64, cols), BF16),
            pltpu.VMEM((2, 2, 4, 32, cols), BF16),
            pltpu.VMEM((2, 2, 4, 64, cols), BF16),
            pltpu.VMEM((2, 2, 32, cols), BF16),
            pltpu.VMEM((2, 2, 64, cols), BF16),
            pltpu.VMEM((64, cols), F32),
            pltpu.VMEM((FACTOR, 64, 256), BF16),
            pltpu.VMEM((64, cols), BF16),
            pltpu.VMEM((n, 8, 16, PART_COLS), BF16),
            pltpu.VMEM((n, 8, 16, PART_COLS), BF16),
            pltpu.VMEM((n, 8, 16, PART_COLS), BF16),
            pltpu.VMEM((4, 4, 64, cols), BF16),
            pltpu.VMEM((cols, wide), BF16),
            pltpu.VMEM((16 * ADAPTER_RANK, cols), BF16),
            pltpu.VMEM((256 * ADAPTER_RANK, wide), BF16),
            pltpu.VMEM((n, 8, 2 * BATCH_ROWS, wide), BF16),
            pltpu.VMEM((n, 8, 2 * BATCH_ROWS, wide), BF16),
            pltpu.VMEM((8, ADAPTER_RANK, 128), F32),
            pltpu.VMEM((8, ADAPTER_RANK, 128), F32),
            pltpu.VMEM((16, ADAPTER_RANK, 128), F32),
            dma(13), dma(11), dma(n, 4), dma(n, 4), dma(n, 2, 4), dma(n, 2), dma(n), dma(n), dma(n),
            dma(n, 2), dma(n), dma(n, 4), dma(n, 4), dma(n), dma(1), dma(1),
        ],
        compiler_params=pltpu.CompilerParams(
            collective_id=0, has_side_effects=True, vmem_limit_bytes=63 * 1024 * 1024
        ),
        name="layer",
    )(
        tokens.reshape(2, 2, 32, width), gate_int_codes, up_int_codes, down_int_codes, shrink, expand,
        gate_column_scale.reshape(-1, 128), up_column_scale.reshape(-1, 128), down_column_scale.reshape(-1, 128),
        row_adapter_index.reshape(8, 128),
    )


def solution(mesh):
    return jax.shard_map(
        body,
        mesh=mesh,
        in_specs=(
            P("tensor", "dp"), P("dp", "tensor"), P("dp", "tensor"), P("tensor", "dp"), P("tensor"), P("tensor"),
            P("dp"), P(), P("dp", "tensor", None), P(None, None, "dp"),
        ),
        out_specs=P("tensor", "dp"),
        check_vma=False,
    )
```

```python
import math

import jax
import jax.numpy as jnp
import numpy as np
from jax import lax
from jax.experimental import pallas as pl
from jax.experimental.pallas import tpu as pltpu
from jax.sharding import PartitionSpec as P

FACTOR = 13
ADAPTER_RANK = 16
MESH = pl.DeviceIdType.MESH
F32, BF16 = jnp.float32, jnp.bfloat16


def sylvester_signs(order):
    i = np.arange(order)
    common = i[:, None] & i[None, :]
    parity = np.zeros_like(common)
    while common.any():
        parity ^= common & 1
        common = common >> 1
    return 1 - 2 * parity


def hartley_entries(order):
    i = np.arange(order)
    angle = 2.0 * np.pi * ((i[:, None] * i[None, :]) % order) / order
    return (np.cos(angle) + np.sin(angle)) / math.sqrt(order)


def order_of(j):
    return (2 - j + (j // 2) * (7 - 2 * j)) % 4


BATCHES = 2
BATCH_ROWS = 64 // BATCHES
HALF_ROWS = BATCH_ROWS // 2
PART_SPLIT = 8 // (BATCH_ROWS // 16)
PART_COLS = {2: 1664, 4: 896}[PART_SPLIT]


def part_place(t):
    j = t % PART_SPLIT
    first = 1664 * j if PART_SPLIT == 2 else 128 * (6 * j + (j + 2) // 3)
    return t // PART_SPLIT, first


def each(count, do):
    lax.fori_loop(0, count, lambda i, carry: (do(i), carry)[1], 0)


def layer_kernel(
    tok, wg_hbm, wu_hbm, wd_hbm, shrink_hbm, expand_hbm, sg_hbm, su_hbm, sd_hbm, ids_hbm, out,
    sgv, suv, sdv, ids, scales, signs, owner, xb, wg, wu, p, r1, r2, t1, t2, hid, mid, loc, am, bm, cm, rot, wd, ws, we, bs, bsr, sp, spr, spd,
    load_sem, send_sem, gr, far_r, near_r, t1_r, t2_r, a_r, c_r, g1_r, g1x_r, g2_r, g2x_r, b_r, h_r, d_r,
):
    dp, tensor = lax.axis_index("dp"), lax.axis_index("tensor")
    z, y = dp // 4, dp % 4
    x, core = tensor // 2, tensor % 2
    cols = wg.shape[1]

    def at_x(step, c):
        return (dp, ((x + step) % 4) * 2 + c)

    def at_z(step):
        return (((z + step) % 4) * 4 + y, tensor)

    def at_y(step):
        return (z * 4 + (y + step) % 4, tensor)

    def peer(i):
        return ((x + i // 2) % 4) * 2 + (core + i % 2) % 2

    def before(i):
        return ((x + 4 - i // 2) % 4) * 2 + (core + i % 2) % 2

    far_first = (4, 5, 2, 3, 6, 7, 1)

    pairs = [(tok.at[q, h], xb.at[x, 2 * core + h, pl.ds(32 * q, 32)]) for q in range(2) for h in range(2)]
    pairs += [(wg_hbm, wg), (wu_hbm, wu), (sg_hbm, sgv), (su_hbm, suv), (sd_hbm, sdv), (ids_hbm, ids)]
    pairs += [(wd_hbm, wd), (shrink_hbm, ws), (expand_hbm, we)]
    loads = [pltpu.make_async_copy(a, b, load_sem.at[i]) for i, (a, b) in enumerate(pairs)]
    near = [at_x(i // 2, (core + i % 2) % 2) for i in range(1, 8)]
    others = [(((z + i // 4) % 4) * 4 + (y + i % 4) % 4, tensor) for i in (10, 6, 9, 11, 14, 2, 5, 7, 8, 13, 15, 1, 3, 4, 12)]
    near += others
    barrier = pltpu.get_barrier_semaphore()
    for who in near:
        pl.semaphore_signal(barrier, inc=1, device_id=who, device_id_type=MESH)
    for load in loads[:10]:
        load.start()
    pl.semaphore_wait(barrier, len(near))

    def remote(src, dst, send, recv, who):
        return pltpu.make_async_remote_copy(
            src_ref=src, dst_ref=dst, send_sem=send, recv_sem=recv, device_id=who, device_id_type=MESH
        )

    mate = at_x(0, 1 - core)
    def shard(q, step, c):
        return xb.at[(x + step) % 4, pl.ds(2 * c, 2), pl.ds(32 * q, 32)]

    def await_bytes(ref, sem):
        remote(ref, ref, send_sem.at[0], sem, mate).wait_recv()

    def gather_copy(q, i, src, dst, who):
        return remote(src, dst, send_sem.at[0 if 0 < i < 4 else 1], gr.at[q, i % 4 if i < 4 else 0], who)

    def gather_start(q):
        for step in (2, 1, 3):
            gather_copy(q, step, tok.at[q], shard(q, 0, core), at_x(step, core)).start()
        gather_copy(q, 0, tok.at[q], shard(q, 0, core), mate).start()

    def gather_mate(q):
        for step in (1, 3, 2):
            ref = shard(q, 4 - step, core)
            await_bytes(ref, gr.at[q, step])
            gather_copy(q, 4, ref, ref, mate).start()

    def gather_end(q):
        await_bytes(xb.at[0], gr.at[q, 0])

    first, second = (z, y), (y, z)
    along = ((at_z, at_y), (at_y, at_z))

    def rows(q, h):
        return pl.ds(pl.multiple_of(BATCH_ROWS * q + HALF_ROWS * h, HALF_ROWS), HALF_ROWS)

    def batch_rows(q):
        return pl.ds(BATCH_ROWS * q, BATCH_ROWS)

    def half_rows(q):
        return pl.ds(HALF_ROWS * q, HALF_ROWS)

    def stage1(q, m, s, kind, k):
        step = 1 + 2 * s
        b = (second[m] + order_of(k)) % 4
        a = (first[m] + (2 if kind == 0 else step)) % 4
        h = 1 - s if kind == 1 else s
        src = p.at[m, a, b, rows(q, h)]
        dst = r1.at[m, s, b, half_rows(q)] if kind == 0 else r2.at[m, s, b, rows(q, h)]
        sem = far_r.at[q, k] if kind == 0 else near_r.at[q, m, k]
        return remote(src, dst, send_sem.at[2], sem, along[m][0](step))

    def stage2(q, m, s, kind):
        step = 1 + 2 * s
        b = (second[m] + (2 if kind == 0 else step)) % 4
        h = 1 - s if kind == 1 else s
        src = p.at[m, first[m], b, rows(q, h)]
        dst = t1.at[m, s, half_rows(q)] if kind == 0 else t2.at[m, s, rows(q, h)]
        sem = t1_r.at[q, s] if kind == 0 else t2_r.at[q]
        return remote(src, dst, send_sem.at[3], sem, along[m][1](step))

    def send_far(q, low=0, high=4):
        @pl.loop(low, high)
        def _(k):
            for m in range(2):
                for s in range(2):
                    stage1(q, m, s, 0, k).start()

    def send_near(q, s):
        @pl.loop(0, 4)
        def _(k):
            for m in range(2):
                stage1(q, m, s, 1, k).start()

    def chunk(q, j):
        for m, w in ((0, wg), (1, wu)):
            a = (first[m] + order_of(j)) % 4
            r = batch_rows(q)
            xs = (xb[a, :, r] if m == 0 else xb[:, a, r]).reshape(4 * BATCH_ROWS, xb.shape[-1])
            for n in range(cols // 256):
                block = slice(n * 256, n * 256 + 256)
                v = jnp.dot(xs, w[:, block], preferred_element_type=F32).astype(BF16)
                p[m, a, :, r, block] = v.reshape(4, BATCH_ROWS, 256)

    def first_batch(j):
        chunk(0, j)

        @pl.when(j == 0)
        def _():
            send_far(0)

        @pl.when((j == 1) | (j == 2))
        def _():
            send_near(0, j - 1)

    def second_batch(j):
        chunk(1, j)

    def mark_owners():
        own_ids = jnp.broadcast_to(ids_of(tensor), (128, 128)).astype(F32).T
        lane_adapter = (lax.broadcasted_iota(jnp.int32, (128, 128), 1) // ADAPTER_RANK).astype(F32)
        spot = own_ids - lane_adapter
        for j in range(32):
            owner[:, j * 128 : j * 128 + 128] = jnp.where(spot == float(8 * j), 1.0, 0.0).astype(BF16)

    def spread_scales():
        lanes = lax.broadcasted_iota(jnp.int32, (256, 256), 0) & lax.broadcasted_iota(jnp.int32, (256, 256), 1)
        for shift in (4, 2, 1):
            lanes = lanes ^ (lanes >> shift)
        signs[...] = (1 - 2 * (lanes & 1)).astype(F32).astype(BF16)
        for i in range(cols // 128):
            for m, ref in enumerate((sgv, suv)):
                scales[m, :, i * 128 : i * 128 + 128] = ref[i : i + 1, :]

    def add(dst, *refs):
        def group(i):
            r = pl.ds(pl.multiple_of(i * 16, 16), 16)
            v = dst[r, :].astype(F32)
            for ref in refs:
                v = v + ref[r, :].astype(F32)
            dst[r, :] = v.astype(BF16)

        each(dst.shape[0] // 16, group)

    def relay(q, k):
        await_bytes(r1.at[:, :, 0, half_rows(q)], far_r.at[q, k])
        for m in range(2):
            for s in range(2):
                b = (second[m] + order_of(k)) % 4
                add(p.at[m, (first[m] + 1 + 2 * s) % 4, b, rows(q, s)], r1.at[m, s, b, half_rows(q)])
                stage1(q, m, s, 2, k).start()

    def settle(q, m, k):
        b = (second[m] + order_of(k)) % 4
        r = batch_rows(q)
        await_bytes(r2.at[m, :, b, r], near_r.at[q, m, k])
        add(p.at[m, first[m], b, r], r2.at[m, 0, b, r], r2.at[m, 1, b, r])

    def cross_far(q):
        for m in range(2):
            settle(q, m, 0)
            for s in range(2):
                stage2(q, m, s, 0).start()

    def cross_near(q):
        for s in range(2):
            for m in range(2):
                settle(q, m, 1 + s)
                stage2(q, m, s, 1).start()

    def cross_relay(q):
        for s in range(2):
            await_bytes(t1.at[:, s, half_rows(q)], t1_r.at[q, s])
            for m in range(2):
                b = (second[m] + 1 + 2 * s) % 4
                add(p.at[m, first[m], b, rows(q, s)], t1.at[m, s, half_rows(q)])
                stage2(q, m, s, 2).start()

    def cross_end(q):
        for m in range(2):
            settle(q, m, 3)
        await_bytes(t2.at[:, :, batch_rows(q)], t2_r.at[q])

    coef = hartley_entries(FACTOR) / math.sqrt(2048)
    def local_part(q):
        def gated(i):
            r = pl.ds(pl.multiple_of(BATCH_ROWS * q + i * 16, 16), 16)
            g, u = (
                p[m, first[m], second[m], r, :].astype(F32) + t2[m, 0, r, :].astype(F32) + t2[m, 1, r, :].astype(F32)
                for m in range(2)
            )
            g, u = g * scales[0], u * scales[1]
            hid[r, :] = g / (1.0 + jnp.exp(-g)) * u

        each(BATCH_ROWS // 16, gated)

        def factor(i):
            r = pl.ds(pl.multiple_of(BATCH_ROWS * q + i * 16, 16), 16)
            blocks = [hid[r, a * 256 : a * 256 + 256] for a in range(FACTOR)]
            for b in range(FACTOR):
                v = blocks[0] * float(coef[b, 0])
                for a in range(1, FACTOR):
                    v = v + blocks[a] * float(coef[b, a])
                mid[b, r, :] = v.astype(BF16)

        each(BATCH_ROWS // 16, factor)
        r = batch_rows(q)
        turned = jnp.dot(
            mid[:, r, :].reshape(FACTOR * BATCH_ROWS, 256), signs[...], preferred_element_type=F32
        ).astype(BF16)
        for b in range(FACTOR):
            loc[r, b * 256 : b * 256 + 256] = turned[b * BATCH_ROWS : (b + 1) * BATCH_ROWS]
        for i in far_first:
            mix_copy(q, i).start()
        am[q, tensor] = my_part(q, tensor)[...]

    def my_part(q, t):
        group, start = part_place(t)
        r = pl.ds(pl.multiple_of(BATCH_ROWS * q + 16 * group, 16), 16)
        return loc.at[r, pl.ds(pl.multiple_of(start, 128), PART_COLS)]

    def mix_copy(q, i):
        to = peer(i)
        return remote(my_part(q, to), am.at[q, tensor], send_sem.at[4], a_r.at[q], (dp, to))

    def back_copy(q, i):
        to = peer(i)
        return remote(bm.at[q, to], cm.at[q, tensor], send_sem.at[5], c_r.at[q], (dp, to))

    def mix(q):
        await_bytes(am.at[q, pl.ds(0, 7)], a_r.at[q])
        for c in range(PART_COLS // 128):
            lane = slice(c * 128, c * 128 + 128)
            v = [am[q, t, :, lane].astype(F32) for t in range(8)]
            for bit in (1, 2, 4):
                v = [v[t] + v[t ^ bit] if t & bit == 0 else v[t ^ bit] - v[t] for t in range(8)]
            for t in range(8):
                bm[q, t, :, lane] = v[t].astype(BF16)
        for i in far_first:
            back_copy(q, i).start()
        cm[q, tensor] = bm[q, tensor]

    def off(c):
        return c + (c // 2) * (5 - 2 * c)

    def held(q, f, c1, c2):
        c = (c1 % 4, c2 % 4) if f == 0 else (c2 % 4, c1 % 4)
        return rot.at[c[0], c[1], rows(q, f)]

    def half_cols(s):
        return pl.ds(s * (cols // 2), cols // 2)

    def spread1(q, f, s, kind):
        step = 1 + 2 * s
        ref = held(q, f, first[f] + (0 if kind == 0 else 4 - step), second[f])
        if kind == 1:
            ref = ref.at[:, half_cols(s)]
        sem = g1_r.at[q, s] if kind == 0 else g1x_r.at[q]
        return remote(ref, ref, send_sem.at[6], sem, along[f][0](step))

    def spread2(q, f, s, kind, c):
        step = 1 + 2 * s
        ref = held(q, f, first[f] + off(c), second[f] + (0 if kind == 0 else 4 - step))
        if kind == 1:
            ref = ref.at[:, half_cols(s)]
        sem = g2_r.at[q, c] if kind == 0 else g2x_r.at[q, c]
        return remote(ref, ref, send_sem.at[7], sem, along[f][1](step))

    def spread_start(q):
        await_bytes(cm.at[q, pl.ds(0, 7)], c_r.at[q])
        for t in range(8):
            group, start = part_place(t)
            r = pl.ds(BATCH_ROWS * q + 16 * group, 16)
            rot[z, y, r, start : start + PART_COLS] = cm[q, t]
        for f in range(2):
            for s in range(2):
                spread1(q, f, s, 0).start()
        for f in range(2):
            for s in range(2):
                spread2(q, f, s, 0, 0).start()

    def spread_mid(q):
        for s in range(2):
            await_bytes(rot.at[0, 0, batch_rows(q)], g1_r.at[q, s])
            for f in range(2):
                spread1(q, f, s, 1).start()
        for s in range(2):
            for f in range(2):
                for s2 in range(2):
                    spread2(q, f, s2, 0, 2 - s).start()

    def spread_far(q):
        await_bytes(rot.at[0, 0, batch_rows(q)], g1x_r.at[q])
        for f in range(2):
            for s2 in range(2):
                spread2(q, f, s2, 0, 3).start()

    def spread_relay(q, c):
        await_bytes(rot.at[0, 0], g2_r.at[q, c])
        for f in range(2):
            for s in range(2):
                spread2(q, f, s, 1, c).start()

    def spread_end(q):
        for c in range(4):
            await_bytes(rot.at[0, 0, batch_rows(q)], g2x_r.at[q, c])

    def sum_piece(q, c1, c2):
        to = 2 * c1 + c2 // 2
        r = pl.ds(pl.multiple_of(BATCH_ROWS * (c2 % 2), BATCH_ROWS), BATCH_ROWS)
        return remote(bs.at[q, to, r], bsr.at[q, tensor, r], send_sem.at[8], b_r.at[q], (dp, to)), to, r

    def ids_of(t):
        row = ids[0:1, :]
        for i in range(1, 8):
            row = jnp.where(t == i, ids[i : i + 1, :], row)
        return row

    lane = lax.broadcasted_iota(jnp.int32, (ADAPTER_RANK, 128), 1)

    def shrink(q, g):
        lhs = rot[pl.ds(2 * g, 2), :, batch_rows(q), :].reshape(8 * BATCH_ROWS, cols)
        both = lax.dot_general(ws[...], lhs, (((1,), (1,)), ((), ())), preferred_element_type=F32)
        for i in range(2):
            parts = both[:, i * 128 : i * 128 + 128]
            even, odd = 4 * g + 2 * i, 4 * g + 2 * i + 1
            if q == 0:
                id_row = jnp.where(lane[:1] < 64, ids_of(even), pltpu.roll(ids_of(odd), 64, 1))
            else:
                id_row = jnp.where(lane[:1] < 64, pltpu.roll(ids_of(even), 64, 1), ids_of(odd))
            v = jnp.zeros((ADAPTER_RANK, 128), F32)
            for a in range(16):
                v = v + jnp.where(id_row == dp * 16 + a, parts[a * 16 : a * 16 + 16], 0.0)
            turned = pltpu.roll(v, 64, 1)
            if q == 0:
                sp[even] = v
                sp[odd] = turned
            else:
                sp[even] = jnp.where(lane < 64, sp[even], turned)
                sp[odd] = jnp.where(lane < 64, sp[odd], v)

    def shrink_all(q):
        for g in range(2):
            shrink(q, g)

    def shrink_send():
        for i in far_first:
            shrink_copy(i).start()

    def down(q, places):
        places = [((z + i) % 4, (y + j) % 4) for i, j in places]
        lhs = jnp.concatenate([rot[c1, c2, batch_rows(q)] for c1, c2 in places], axis=0)
        base = jnp.dot(lhs, wd[...], preferred_element_type=F32).astype(BF16)
        for n, (c1, c2) in enumerate(places):
            copy, to, r = sum_piece(q, c1, c2)
            bs[q, to, r] = base[n * BATCH_ROWS : (n + 1) * BATCH_ROWS]

            @pl.when(to != tensor)
            def _():
                copy.start()

    def down_early(q):
        down(q, [(i, j) for j in (0, 1, 3) for i in (0, 1, 3)])

    def down_late(q):
        down(q, [(2, j) for j in range(4)] + [(i, 2) for i in (0, 1, 3)])

    def shrink_copy(i):
        to = peer(i)
        return remote(sp.at[to], spr.at[tensor], send_sem.at[9], h_r.at[0], (dp, to))

    def shrink_across(who):
        return remote(spd.at[dp], spd.at[dp], send_sem.at[10], d_r.at[0], who)

    def total(refs):
        v = refs[0]
        for ref in refs[1:]:
            v = v + ref
        return v

    def finish():
        await_bytes(spr.at[pl.ds(0, 7)], h_r.at[0])
        spr[tensor] = sp[tensor]
        spd[dp] = total([spr[t] for t in range(8)])
        for who in others:
            shrink_across(who).start()
        bases = []
        for q in range(BATCHES):
            await_bytes(bsr.at[q, pl.ds(0, 7)], b_r.at[q])
            bsr[q, tensor] = bs[q, tensor]
            bases.append(total([bsr[q, t].astype(F32) for t in range(8)]))
        await_bytes(spd.at[pl.ds(0, 15)], d_r.at[0])
        shrunk = total([spd[c] for c in range(16)])
        wide = jnp.concatenate([shrunk] * 8, axis=0).T
        chosen = owner[...] * jnp.concatenate([wide.astype(BF16)] * 32, axis=1)
        extra = jnp.dot(chosen, we[...], preferred_element_type=F32)
        for q in range(BATCHES):
            r = slice(2 * BATCH_ROWS * q, 2 * BATCH_ROWS * (q + 1))
            base = bases[q]
            for i in range(out.shape[1] // 128):
                block = slice(i * 128, i * 128 + 128)
                out[r, block] = (base[:, block] * sdv[i : i + 1, :] + extra[r, block]).astype(BF16)

    gather_start(0)
    gather_mate(0)
    for load in loads[:6]:
        load.wait()
    gather_end(0)
    gather_start(1)
    each(4, first_batch)
    gather_mate(1)
    gather_end(1)
    for load in loads[10:]:
        load.start()
    each(4, second_batch)
    for load in loads[6:10]:
        load.wait()
    spread_scales()
    send_far(1, 0, 2)
    relay(0, 0)
    relay(0, 1)
    relay(0, 2)
    relay(0, 3)
    cross_far(0)
    cross_near(0)
    relay(1, 0)
    relay(1, 1)
    send_far(1, 2, 4)
    cross_relay(0)
    send_near(1, 0)
    send_near(1, 1)
    relay(1, 2)
    cross_end(0)
    relay(1, 3)
    cross_far(1)
    local_part(0)
    cross_near(1)
    mix(0)
    cross_relay(1)
    spread_start(0)
    cross_end(1)
    local_part(1)
    spread_mid(0)
    mix(1)
    spread_far(0)
    spread_relay(0, 1)
    spread_relay(0, 0)
    spread_relay(0, 2)
    spread_start(1)
    mark_owners()
    for load in loads[10:]:
        load.wait()
    spread_relay(0, 3)
    spread_mid(1)
    down_early(0)
    spread_end(0)
    spread_far(1)
    shrink_all(0)
    spread_relay(1, 1)
    down_late(0)
    spread_relay(1, 2)
    spread_relay(1, 0)
    spread_relay(1, 3)
    down_early(1)
    spread_end(1)
    shrink_all(1)
    shrink_send()
    down_late(1)
    finish()

    gone = (
        xb.at[pl.ds(0, 2), pl.ds(0, 3)], xb.at[pl.ds(0, 2)], p.at[:, pl.ds(0, 3)], p.at[0, pl.ds(0, 2), pl.ds(0, 3)],
        am.at[:, pl.ds(0, 7)], cm.at[:, pl.ds(0, 7)], rot.at[0, pl.ds(0, 3)], rot.at[pl.ds(0, 3)],
        bs.at[:, pl.ds(0, 7)], sp.at[pl.ds(0, 7)], spd.at[pl.ds(0, 15)],
    )
    for i, ref in enumerate(gone):
        remote(ref, ref, send_sem.at[i], h_r.at[0], mate).wait_send()


def body(
    tokens, gate_int_codes, up_int_codes, down_int_codes, gate_column_scale, up_column_scale, down_column_scale,
    row_adapter_index, adapter_shrink_weight, adapter_expand_weight,
):
    rows, width = tokens.shape
    cols, wide = down_int_codes.shape
    shrink = jnp.transpose(adapter_shrink_weight, (0, 2, 1)).reshape(-1, cols)
    expand = adapter_expand_weight.reshape(-1, wide)
    vmem = pl.BlockSpec(memory_space=pltpu.VMEM)
    hbm = pl.BlockSpec(memory_space=pl.ANY)

    def dma(*shape):
        return pltpu.SemaphoreType.DMA(shape)

    n = BATCHES
    return pl.pallas_call(
        layer_kernel,
        out_shape=pltpu.VMEM((rows, wide), BF16),
        in_specs=[hbm] * 10,
        out_specs=vmem,
        scratch_shapes=[
            pltpu.VMEM((cols // 128, 128), F32),
            pltpu.VMEM((cols // 128, 128), F32),
            pltpu.VMEM((wide // 128, 128), F32),
            pltpu.VMEM((8, 128), jnp.int32),
            pltpu.VMEM((2, 1, cols), F32),
            pltpu.VMEM((256, 256), BF16),
            pltpu.VMEM((128, 256 * ADAPTER_RANK), BF16),
            pltpu.VMEM((4, 4, 64, width), BF16),
            pltpu.VMEM((width, cols), BF16),
            pltpu.VMEM((width, cols), BF16),
            pltpu.VMEM((2, 4, 4, 64, cols), BF16),
            pltpu.VMEM((2, 2, 4, 32, cols), BF16),
            pltpu.VMEM((2, 2, 4, 64, cols), BF16),
            pltpu.VMEM((2, 2, 32, cols), BF16),
            pltpu.VMEM((2, 2, 64, cols), BF16),
            pltpu.VMEM((64, cols), F32),
            pltpu.VMEM((FACTOR, 64, 256), BF16),
            pltpu.VMEM((64, cols), BF16),
            pltpu.VMEM((n, 8, 16, PART_COLS), BF16),
            pltpu.VMEM((n, 8, 16, PART_COLS), BF16),
            pltpu.VMEM((n, 8, 16, PART_COLS), BF16),
            pltpu.VMEM((4, 4, 64, cols), BF16),
            pltpu.VMEM((cols, wide), BF16),
            pltpu.VMEM((16 * ADAPTER_RANK, cols), BF16),
            pltpu.VMEM((256 * ADAPTER_RANK, wide), BF16),
            pltpu.VMEM((n, 8, 2 * BATCH_ROWS, wide), BF16),
            pltpu.VMEM((n, 8, 2 * BATCH_ROWS, wide), BF16),
            pltpu.VMEM((8, ADAPTER_RANK, 128), F32),
            pltpu.VMEM((8, ADAPTER_RANK, 128), F32),
            pltpu.VMEM((16, ADAPTER_RANK, 128), F32),
            dma(13), dma(11), dma(n, 4), dma(n, 4), dma(n, 2, 4), dma(n, 2), dma(n), dma(n), dma(n),
            dma(n, 2), dma(n), dma(n, 4), dma(n, 4), dma(n), dma(1), dma(1),
        ],
        compiler_params=pltpu.CompilerParams(
            collective_id=0, has_side_effects=True, vmem_limit_bytes=63 * 1024 * 1024
        ),
        name="layer",
    )(
        tokens.reshape(2, 2, 32, width), gate_int_codes, up_int_codes, down_int_codes, shrink, expand,
        gate_column_scale.reshape(-1, 128), up_column_scale.reshape(-1, 128), down_column_scale.reshape(-1, 128),
        row_adapter_index.reshape(8, 128),
    )


def solution(mesh):
    return jax.shard_map(
        body,
        mesh=mesh,
        in_specs=(
            P("tensor", "dp"), P("dp", "tensor"), P("dp", "tensor"), P("tensor", "dp"), P("tensor"), P("tensor"),
            P("dp"), P(), P("dp", "tensor", None), P(None, None, "dp"),
        ),
        out_specs=P("tensor", "dp"),
        check_vma=False,
    )
```
